128 devices in a mesh: row: 16 (over y, z_lo, core), col: 8 (over x, z_hi).
Axes of the slice: x: 4, y: 4, z: 4 (z_hi: 2, z_lo: 2; z = z_hi * 2 + z_lo), core: 2. Of those that a mesh axis runs over, the one named last changes fastest.
Arguments:
- queries: bfloat16 [16, 96, 48, 1536], P(None, 'row', 'col')
- keys: bfloat16 [16, 96, 48, 1536], P(None, 'row', 'col')
- values: bfloat16 [16, 96, 48, 1536], P(None, 'row', 'col'), may hold values from -6 to 6
- tokens: bfloat16 [16, 96, 48, 3072], P(None, 'row', 'col'), may hold values from -6 to 6
- out_weight: bfloat16 [1536, 3072], replicated, may hold values from -0.15625 to 0.15625
- proj_weight: bfloat16 [3072, 512], replicated, may hold values from -0.109375 to 0.109375
- conv_weight: bfloat16 [13824, 512], P('row'), may hold values from -0.0546875 to 0.0546875
Outputs:
- upsampled: bfloat16 [16, 192, 96, 128], P('row', 'col')
The draws below stay inside these ranges and needn't reach their ends.
All inputs are finite; a program needn't handle non-finite values.
Results may differ from the reference program's by a relative error of at most 0.0058.
Values may be sent and summed in bfloat16 or wider, within the bound.
A program may use at most 192 MiB of HBM per device.

```python
import math
import jax
import jax.numpy as jnp
from jax import lax

D = 3072
HEADS = 12
HEAD_DIM = 128
CH = 512
TH = 6
INNER = 1536
CQ = 128
SH = 3
FRAMES = 16
HH = 96
WW = 48
N_ROW = 16
N_COL = 8


def drawn_keys(key):
    base = jax.random.normal(jax.random.fold_in(key, 11), (FRAMES, HH, WW, INNER), jnp.float32)
    return base


def draw_keys(key, part):
    base = drawn_keys(key)
    return base.astype(jnp.bfloat16)


def draw_queries(key, part):
    key = jax.random.fold_in(key, 4)
    result = jax.random.normal(jax.random.fold_in(key, 1), (FRAMES, HH, WW, INNER), jnp.float32)
    return result.astype(jnp.bfloat16)


def levels(own_key, dims, cuts, smallest, high):
    gain, own = 1.0, jax.random.fold_in(own_key, 6)
    for axis_at, blocks in cuts:
        heights = jnp.exp(jax.random.uniform(jax.random.fold_in(own, axis_at), (blocks,), jnp.float32, smallest / len(cuts), high / len(cuts)))
        gain = gain * jnp.repeat(heights, dims[axis_at] // blocks).reshape([-1 if axis == axis_at else 1 for axis in range(len(dims))])
    return gain


def scatter_about(rng, dims, spread, bound, pieces=(), dtype=jnp.bfloat16):
    loudness = levels(rng, dims, pieces, -0.22, 0.18) if pieces else 1.0
    array = jax.random.normal(rng, dims, jnp.float32) * spread * loudness
    return jnp.minimum(jnp.maximum(array, -bound), bound).astype(dtype)


def setup_inputs(seed: int = 0) -> dict:
    key_of = jax.random.split(jax.random.key(seed), 8)
    queries = draw_queries(jax.random.fold_in(key_of[7], 71), 0)
    keys = draw_keys(jax.random.fold_in(key_of[7], 71), 0)
    values = scatter_about(key_of[2], (FRAMES, HH, WW, INNER), 1.0, 6.0, ((1, 16), (2, 8)))
    tokens = scatter_about(key_of[3], (FRAMES, HH, WW, D), 1.0, 6.0, ((1, 16), (2, 8)))
    out_weight = scatter_about(key_of[4], (INNER, D), INNER ** -0.5, 0.15625)
    proj_weight = scatter_about(key_of[5], (D, CH), D ** -0.5, 0.109375)
    conv_weight = scatter_about(key_of[6], (27 * CH, CH), (27 * CH) ** -0.5, 0.0546875, ((0, 16),))
    return {"queries": queries, "keys": keys, "values": values, "tokens": tokens, "out_weight": out_weight, "proj_weight": proj_weight, "conv_weight": conv_weight}


def attend_window(query_rows, key_rows, value_rows):
    count = query_rows.shape[0]
    query_heads = query_rows.astype(jnp.float32).reshape(count, HEADS, HEAD_DIM)
    key_heads = key_rows.astype(jnp.float32).reshape(count, HEADS, HEAD_DIM)
    value_heads = value_rows.astype(jnp.float32).reshape(count, HEADS, HEAD_DIM)
    scores = jnp.einsum('qhd,khd->hqk', query_heads, key_heads) / math.sqrt(HEAD_DIM)
    highest = lax.optimization_barrier(jnp.max(scores, axis=-1, keepdims=True))
    weights = jnp.exp(scores - highest)
    probs = (weights / lax.optimization_barrier(jnp.sum(weights, axis=-1, keepdims=True))).astype(jnp.bfloat16)
    mixed = jnp.einsum('hqk,khd->qhd', probs.astype(jnp.float32), value_heads)
    return mixed.astype(jnp.bfloat16).reshape(count, HEADS * HEAD_DIM)

def to_windows(field):
    rolled = jnp.roll(field, (-SH, -SH), axis=(1, 2))
    depth = field.shape[-1]
    blocks = rolled.reshape(FRAMES, N_ROW, TH, N_COL, TH, depth).transpose(1, 3, 0, 2, 4, 5)
    return blocks.reshape(N_ROW * N_COL, FRAMES * TH * TH, depth)

def layer_window(inputs):
    query_rows, key_rows, value_rows, token_rows, out_weight, proj_weight = inputs
    attended = attend_window(query_rows, key_rows, value_rows)
    residual = token_rows.astype(jnp.float32) + jnp.dot(attended, out_weight, preferred_element_type=jnp.float32)
    normed = (residual * lax.rsqrt(lax.optimization_barrier(jnp.mean(residual * residual, axis=-1, keepdims=True)) + 1e-06)).astype(jnp.bfloat16)
    return jax.nn.silu(jnp.dot(normed, proj_weight, preferred_element_type=jnp.float32)).astype(jnp.bfloat16)

def reference(queries, keys, values, tokens, out_weight, proj_weight, conv_weight):
    wq = to_windows(queries)
    wk = to_windows(keys)
    wv = to_windows(values)
    wt = to_windows(tokens)
    per_window = lax.map(lambda items: layer_window((items[0], items[1], items[2], items[3], out_weight, proj_weight)), (wq, wk, wv, wt))
    grid = per_window.reshape(N_ROW, N_COL, FRAMES, TH, TH, CH).transpose(2, 0, 3, 1, 4, 5).reshape(FRAMES, HH, WW, CH)
    features = jnp.roll(grid, (SH, SH), axis=(1, 2))
    padded = jnp.pad(features, ((2, 0), (1, 1), (1, 1), (0, 0)))

    def one_frame(index):
        block = lax.dynamic_slice_in_dim(padded, index.astype(jnp.int32), 3, 0)
        patches = jnp.concatenate([block[step_t, off_y:off_y + HH, off_x:off_x + WW] for step_t in range(3) for off_y in range(3) for off_x in range(3)], axis=-1)
        patches = patches.reshape(HH * WW, 27 * CH)
        conv_out = jnp.dot(patches, conv_weight, preferred_element_type=jnp.float32)
        shuffled = conv_out.reshape(HH, WW, CQ, 2, 2).transpose(0, 3, 1, 4, 2).reshape(2 * HH, 2 * WW, CQ)
        return shuffled.astype(jnp.bfloat16)
    return lax.map(one_frame, jnp.arange(FRAMES).astype(jnp.int32))
```

```python
import math

import jax
import jax.numpy as jnp
from jax import lax
from jax.experimental import pallas as pl
from jax.experimental.pallas import tpu as pltpu
from jax.sharding import PartitionSpec as P

MESH = pl.DeviceIdType.MESH
HEADS = 12
HEAD = 128
GROUPS = 6
WIDE = 256
INNER = 1536
D = 3072
CH = 512
SHARD = 864
HALF = 432
ROWS = 576
CHUNK = 512
F32 = jnp.float32
BF16 = jnp.bfloat16


def lanes(start, size):
    return pl.ds(pl.multiple_of(start, 128), size)


def body(q_ref, k_ref, v_ref, t_ref, wo_ref, wp_ref, cw_ref, out_ref,
         win, att, home, res, tok, wo, wp, cw, shard, field, acc, parts, perm, back, sent, got, ssq,
         fs, fr, rs, rr, ls, ws, wr, hs, hr, os_, or_):
    r = lax.axis_index("row")
    c = lax.axis_index("col")
    odd = lax.rem(r, 2)
    x, zh = lax.div(c, 2), lax.rem(c, 2)
    y, zl = lax.div(r, 4), lax.rem(lax.div(r, 2), 2)

    def at(row, col):
        return (lax.rem(row + 16, 16), lax.rem(col + 8, 8))

    def along_x(step):
        return (r, lax.rem(x + step, 4) * 2 + zh)

    def along_y(step):
        return (lax.rem(y + step, 4) * 4 + zl * 2 + odd, c)

    other_zl = (y * 4 + (1 - zl) * 2 + odd, c)
    other_core = (r + 1 - 2 * odd, c)
    forward = (at(r - 1, c - odd), at(r - 1, c + 1 - odd), at(r, c - 1 + 2 * odd))
    homes = (at(r + 1, c + 1 - odd), at(r + 1, c - odd), at(r, c + 1 - 2 * odd))
    around = [(dr, dc) for dr in (-1, 0, 1) for dc in (-1, 0, 1) if (dr, dc) != (0, 0)]
    own_band = lax.div(r, 2) == c

    barrier = pltpu.get_barrier_semaphore()

    def greet(device):
        pl.semaphore_signal(barrier, inc=1, device_id=device, device_id_type=MESH)

    for device in forward + homes:
        greet(device)
    for dr, dc in around:
        greet(at(r + dr, c + dc))
    for step in (1, 2, 3):
        greet(along_x(step))
        greet(along_y(step))
    greet(other_zl)
    greet(other_core)

    def greet_band(i, carry):
        row, col = 2 * c + lax.div(i, 8), lax.rem(i, 8)

        @pl.when(jnp.logical_or(row != r, col != c))
        def _():
            greet((row, col))

        return carry

    lax.fori_loop(0, 16, greet_band, 0)

    local = [
        pltpu.make_async_copy(cw_ref, shard, ls.at[0]),
        pltpu.make_async_copy(t_ref, tok, ls.at[1]),
        pltpu.make_async_copy(wo_ref, wo, ls.at[2]),
        pltpu.make_async_copy(wp_ref, wp, ls.at[3]),
    ]
    sources = (q_ref, k_ref, v_ref)
    for n in range(3):
        local.append(
            pltpu.make_async_copy(
                sources[n].at[pl.ds(3, 3), pl.ds(3 * (1 - odd), 3)], win.at[n, odd], ls.at[4 + n]
            )
        )
    local[0].start()
    for copy in local[4:]:
        copy.start()

    pl.semaphore_wait(barrier, 38 - own_band.astype(jnp.int32))

    def send(g, n, t):
        span = lanes(g * WIDE, WIDE)
        if t == 2:
            src = sources[n].at[pl.ds(3, 3), pl.ds(3 * odd, 3), :, span]
            dst = win.at[n, 1 - odd, :, :, :, span]
        else:
            src = sources[n].at[pl.ds(0, 3), pl.ds(3 * t, 3), :, span]
            dst = win.at[n, 3 - t, :, :, :, span]
        return pltpu.make_async_remote_copy(
            src_ref=src, dst_ref=dst, send_sem=fs.at[g, n, t], recv_sem=fr.at[g, n, t],
            device_id=forward[t], device_id_type=MESH,
        )

    def give(g, t):
        span = lanes(g * WIDE, WIDE)
        if t == 2:
            src = att.at[1 - odd, :, :, :, span]
            dst = home.at[pl.ds(3, 3), pl.ds(3 * odd, 3), :, span]
        else:
            src = att.at[3 - t, :, :, :, span]
            dst = home.at[pl.ds(0, 3), pl.ds(3 * t, 3), :, span]
        return pltpu.make_async_remote_copy(
            src_ref=src, dst_ref=dst, send_sem=rs.at[g, t], recv_sem=rr.at[g, t],
            device_id=homes[t], device_id_type=MESH,
        )

    def keep(g):
        span = lanes(g * WIDE, WIDE)
        return pltpu.make_async_copy(
            att.at[odd, :, :, :, span], home.at[pl.ds(3, 3), pl.ds(3 * (1 - odd), 3), :, span], rr.at[g, 3]
        )

    def send_group(g):
        for n in range(3):
            for t in (2, 0, 1):
                send(g, n, t).start()

    send_group(0)
    send_group(1)
    for copy in local[1:4]:
        copy.start()

    quarter = lanes(x * 128, 128)
    everything = pl.ds(0, CH)

    def piece(i, y_, zl_, part, span, device):
        first, size = part
        start = pl.multiple_of((y_ * 4 + zl_ * 2 + odd) * SHARD + first, 16)
        block = cw.at[pl.ds(start, size), span]
        return pltpu.make_async_remote_copy(
            src_ref=block, dst_ref=block, send_sem=ws.at[i], recv_sem=wr.at[i],
            device_id=device, device_id_type=MESH,
        )

    def whose_y(step):
        return lax.rem(y + step, 4)

    low, high, full = (0, HALF), (HALF, HALF), (0, SHARD)
    stage_0 = [(0, y, zl, full, quarter, other_zl)]
    for s in (1, 2, 3):
        stage_0.append((s, y, zl, low, quarter, along_y(s)))
        stage_0.append((3 + s, y, zl, high, everything, along_y(s)))
    stage_1 = []
    for s in (1, 2, 3):
        stage_1.append((6 + s, y, 1 - zl, low, quarter, along_y(s)))
        stage_1.append((9 + s, y, 1 - zl, high, quarter, along_x(s)))
        stage_1.append((12 + s, y, 1 - zl, low, quarter, along_x(s)))
        for d in (1, 2, 3):
            stage_1.append((12 + 3 * d + s, whose_y(d), zl, low, quarter, along_x(s)))
    stage_2 = []
    for s in (1, 2, 3):
        stage_2.append((24 + s, y, 1 - zl, high, everything, along_y(s)))
        for d in (1, 2, 3):
            stage_2.append((24 + 3 * d + s, whose_y(d), 1 - zl, low, quarter, along_x(s)))
    swap_0 = [(37, y, zl, full, everything, other_core)]
    swap_1 = [(37 + d, whose_y(d), zl, high, everything, other_core) for d in (1, 2, 3)]
    swap_2 = [(41, y, 1 - zl, full, everything, other_core)]
    swap_3 = []
    for d in (1, 2, 3):
        swap_3.append((41 + d, whose_y(d), zl, low, everything, other_core))
        swap_3.append((44 + d, whose_y(d), 1 - zl, full, everything, other_core))

    def start_all(pieces):
        for item in pieces:
            piece(*item).start()

    def wait_all(pieces, which=None):
        for item in pieces:
            if which is None or item[0] in which:
                piece(*item).wait_recv()

    def drain(pieces):
        for item in pieces:
            piece(*item).wait_send()

    local[0].wait()
    key = lax.broadcasted_iota(jnp.int32, (CH, CH), 0)
    lane = lax.broadcasted_iota(jnp.int32, (CH, CH), 1)
    order = jnp.where(key == 4 * (lane & 127) + (lane >> 7), 1.0, 0.0).astype(BF16)
    own_start = pl.multiple_of(r * SHARD, 16)
    for part in range(3):
        cw[pl.ds(own_start + 288 * part, 288), :] = jnp.dot(
            shard[pl.ds(288 * part, 288), :], order, preferred_element_type=F32
        ).astype(BF16)
    start_all(stage_0)
    start_all(swap_0)

    row = lax.broadcasted_iota(jnp.int32, (256, 192), 0)
    col = lax.broadcasted_iota(jnp.int32, (256, 192), 1)
    frame, place = row >> 4, row & 15
    wanted = (place & 1) * 96 + (place >> 1) * 16 + frame
    perm[...] = jnp.where(jnp.logical_and(place < 12, col == wanted), 1.0, 0.0).astype(BF16)
    row = lax.broadcasted_iota(jnp.int32, (96, 128), 0)
    col = lax.broadcasted_iota(jnp.int32, (96, 128), 1)
    which = (row * 171) >> 11
    back[...] = jnp.where(col == which * 16 + row - 12 * which, 1.0, 0.0).astype(BF16)

    for copy in local[4:]:
        copy.wait()

    def attend(h):
        span = lanes(h * HEAD, HEAD)
        keys = win[1, :, :, :, :, span].reshape(ROWS, HEAD)
        values = win[2, :, :, :, :, span].reshape(ROWS, HEAD)
        for part in range(2):
            queries = win[0, pl.ds(2 * part, 2), :, :, :, span].reshape(ROWS // 2, HEAD)
            scores = lax.dot_general(
                queries, keys, (((1,), (1,)), ((), ())), preferred_element_type=F32
            ) * (1.0 / math.sqrt(HEAD))
            highest = jnp.max(scores, axis=-1, keepdims=True)
            weights = jnp.exp(scores - highest)
            probs = (weights * (1.0 / jnp.sum(weights, axis=-1, keepdims=True))).astype(BF16)
            mixed = jnp.dot(probs, values, preferred_element_type=F32).astype(BF16)
            att[pl.ds(2 * part, 2), :, :, :, span] = mixed.reshape(2, 3, 3, 16, HEAD)

    def await_home(g):
        for t in range(3):
            give(g, t).wait_recv()
        keep(g).wait()

    def add_group(g, first):
        rows = home[:, :, :, lanes(g * WIDE, WIDE)].reshape(ROWS, WIDE)

        def chunk(n, carry):
            span = lanes(n * CHUNK, CHUNK)
            product = jnp.dot(
                rows, wo[pl.ds(pl.multiple_of(g * WIDE, WIDE), WIDE), span], preferred_element_type=F32
            )
            base = tok[:, span].astype(F32) if first else res[:, span]
            res[:, span] = base + product
            return carry

        lax.fori_loop(0, D // CHUNK, chunk, 0)

    def group(g, carry):
        for n in range(3):
            for t in range(3):
                send(g, n, t).wait_recv()

        @pl.when(g < GROUPS - 2)
        def _():
            for n in range(3):
                for t in range(3):
                    send(g, n, t).wait_send()
            send_group(g + 2)

        for h in range(WIDE // HEAD):
            attend(g * (WIDE // HEAD) + h)
        for t in (2, 0, 1):
            give(g, t).start()
        keep(g).start()

        @pl.when(g == 0)
        def _():
            wait_all(stage_0)
            start_all(stage_1)
            start_all(swap_1)
            for copy in local[1:4]:
                copy.wait()

        @pl.when(g == 2)
        def _():
            wait_all(stage_1, (7, 8, 9, 10, 11, 12, 13, 14, 15))
            start_all(stage_2)
            start_all(swap_2)

        @pl.when(g == 1)
        def _():
            await_home(0)
            add_group(0, True)

        @pl.when(g > 1)
        def _():
            await_home(g - 1)
            add_group(g - 1, False)

        return carry

    lax.fori_loop(0, GROUPS, group, 0)

    wait_all(stage_1, tuple(range(16, 25)))
    wait_all(stage_2)
    start_all(swap_3)

    last = GROUPS - 1
    await_home(last)
    rows = home[:, :, :, pl.ds(last * WIDE, WIDE)].reshape(ROWS, WIDE)
    ssq[...] = jnp.zeros_like(ssq)
    acc[...] = jnp.zeros_like(acc)

    def finish(n, carry):
        span = lanes(n * CHUNK, CHUNK)
        total = res[:, span] + jnp.dot(rows, wo[pl.ds(last * WIDE, WIDE), span], preferred_element_type=F32)
        ssq[...] += jnp.sum(total * total, axis=-1, keepdims=True)
        acc[...] += jnp.dot(
            total.astype(BF16), wp[pl.ds(pl.multiple_of(n * CHUNK, CHUNK), CHUNK), :], preferred_element_type=F32
        )
        return carry

    lax.fori_loop(0, D // CHUNK, finish, 0)
    raw = acc[...] * lax.rsqrt(ssq[...] * (1.0 / D) + 1e-6)
    features = (raw / (1.0 + jnp.exp(-raw))).astype(BF16)
    field[pl.ds(1, 6), pl.ds(1, 6)] = features.reshape(6, 6, 16, CH)

    def rim(i):
        dr, dc = around[i]
        take = [pl.ds(1, 6) if d == 0 else (1 if d < 0 else 6) for d in (dr, dc)]
        put = [pl.ds(1, 6) if d == 0 else (7 if d < 0 else 0) for d in (dr, dc)]
        return pltpu.make_async_remote_copy(
            src_ref=field.at[take[0], take[1]], dst_ref=field.at[put[0], put[1]],
            send_sem=hs.at[i], recv_sem=hr.at[i],
            device_id=at(r + dr, c + dc), device_id_type=MESH,
        )

    for i in range(8):
        rim(i).start()
    wait_all(swap_0 + swap_1 + swap_2 + swap_3)
    for i in range(8):
        rim(i).wait()

    @pl.when(r == 0)
    def _():
        field[0] = jnp.zeros((8, 16, CH), BF16)

    @pl.when(r == 15)
    def _():
        field[7] = jnp.zeros((8, 16, CH), BF16)

    @pl.when(c == 0)
    def _():
        field[:, 0] = jnp.zeros((8, 16, CH), BF16)

    @pl.when(c == 7)
    def _():
        field[:, 7] = jnp.zeros((8, 16, CH), BF16)

    for dy in range(3):
        for dx in range(3):
            win[dy, :, :, :, :, pl.ds(dx * CH, CH)] = field[pl.ds(dy, 6), pl.ds(dx, 6)].reshape(4, 3, 3, 16, CH)

    def to_frame(a, f):
        return pltpu.make_async_remote_copy(
            src_ref=sent.at[a, f], dst_ref=got.at[a, odd * 8 + c],
            send_sem=os_.at[a, f], recv_sem=or_.at[a, odd * 8 + c],
            device_id=(f, lax.div(r, 2)), device_id_type=MESH,
        )

    def stay(a):
        return pltpu.make_async_copy(sent.at[a, r], got.at[a, odd * 8 + c], or_.at[a, odd * 8 + c])

    def self_is(f):
        return jnp.logical_and(own_band, f == r)

    age = lax.broadcasted_iota(jnp.int32, (ROWS, 256), 0) & 15
    for a in range(2):
        def tap(dt, carry):
            total = jnp.zeros((ROWS, 256), F32)
            for dy in range(3):
                rows_w = pl.ds(pl.multiple_of((dt * 3 + dy) * 3 * CH, 16), 3 * CH)
                total += jnp.dot(
                    win[dy].reshape(ROWS, 3 * CH), cw[rows_w, pl.ds(a * 256, 256)], preferred_element_type=F32
                )
            parts[dt] = total
            return carry

        lax.fori_loop(0, 3, tap, 0)
        conv = parts[2]
        conv += jnp.where(age >= 1, pltpu.roll(parts[1], 1, axis=0), 0.0)
        conv += jnp.where(age >= 2, pltpu.roll(parts[0], 2, axis=0), 0.0)
        done = conv.astype(BF16)
        for i in range(6):
            strip = done[96 * i : 96 * i + 96]
            stacked = jnp.concatenate([strip[:, :128], strip[:, 128:]], axis=0)
            moved = jnp.dot(perm[...], stacked, preferred_element_type=F32).astype(BF16)
            sent[a, :, pl.ds(16 * i, 16), :] = moved.reshape(16, 16, 128)

        def ship(f, carry):
            @pl.when(self_is(f))
            def _():
                stay(a).start()

            @pl.when(jnp.logical_not(self_is(f)))
            def _():
                to_frame(a, f).start()

            return carry

        lax.fori_loop(0, 16, ship, 0)

    def arrival(a, i):
        return pltpu.make_async_remote_copy(
            src_ref=sent.at[a, i], dst_ref=got.at[a, i], send_sem=os_.at[a, i], recv_sem=or_.at[a, i],
            device_id=other_core, device_id_type=MESH,
        )

    for a in range(2):
        def collect(i, carry):
            arrival(a, i).wait_recv()
            return carry

        lax.fori_loop(0, 16, collect, 0)
        for half in range(2):
            for i in range(6):
                block = got[a, pl.ds(8 * half, 8), pl.ds(16 * i, 16), :].reshape(128, 128)
                out_ref[12 * half + 2 * i + a] = jnp.dot(
                    back[...], block, preferred_element_type=F32
                ).astype(BF16)

    def drain_group(g, carry):
        @pl.when(g >= GROUPS - 2)
        def _():
            for n in range(3):
                for t in range(3):
                    send(g, n, t).wait_send()

        for t in range(3):
            give(g, t).wait_send()
        return carry

    lax.fori_loop(0, GROUPS, drain_group, 0)
    drain(stage_0 + stage_1 + stage_2 + swap_0 + swap_1 + swap_2 + swap_3)

    def drain_out(f, carry):
        for a in range(2):
            @pl.when(jnp.logical_not(self_is(f)))
            def _():
                to_frame(a, f).wait_send()

        return carry

    lax.fori_loop(0, 16, drain_out, 0)


def local(queries, keys, values, tokens, out_weight, proj_weight, conv_weight):
    cells = [jnp.transpose(a, (1, 2, 0, 3)) for a in (queries, keys, values)]
    rows = jnp.transpose(tokens, (1, 2, 0, 3)).reshape(ROWS, D)
    anywhere = pl.BlockSpec(memory_space=pl.ANY)
    dma = pltpu.SemaphoreType.DMA
    out = pl.pallas_call(
        body,
        out_shape=jax.ShapeDtypeStruct((24, 96, 128), BF16),
        in_specs=[anywhere] * 7,
        out_specs=pl.BlockSpec(memory_space=pltpu.VMEM),
        scratch_shapes=[
            pltpu.VMEM((3, 4, 3, 3, 16, INNER), BF16),
            pltpu.VMEM((4, 3, 3, 16, INNER), BF16),
            pltpu.VMEM((6, 6, 16, INNER), BF16),
            pltpu.VMEM((ROWS, D), F32),
            pltpu.VMEM((ROWS, D), BF16),
            pltpu.VMEM((INNER, D), BF16),
            pltpu.VMEM((D, CH), BF16),
            pltpu.VMEM((16 * SHARD, CH), BF16),
            pltpu.VMEM((SHARD, CH), BF16),
            pltpu.VMEM((8, 8, 16, CH), BF16),
            pltpu.VMEM((ROWS, CH), F32),
            pltpu.VMEM((3, ROWS, 256), F32),
            pltpu.VMEM((256, 192), BF16),
            pltpu.VMEM((96, 128), BF16),
            pltpu.VMEM((2, 16, 96, 128), BF16),
            pltpu.VMEM((2, 16, 96, 128), BF16),
            pltpu.VMEM((ROWS, 1), F32),
            dma((GROUPS, 3, 3)), dma((GROUPS, 3, 3)),
            dma((GROUPS, 3)), dma((GROUPS, 4)),
            dma((7,)),
            dma((48,)), dma((48,)),
            dma((8,)), dma((8,)),
            dma((2, 16)), dma((2, 16)),
        ],
        compiler_params=pltpu.CompilerParams(
            collective_id=0, has_side_effects=True, vmem_limit_bytes=62 * 1024 * 1024
        ),
    )(*cells, rows, out_weight, proj_weight, conv_weight)
    return out[None]


def solution(mesh):
    tile = P(None, "row", "col", None)
    placed = (tile, tile, tile, tile, P(), P(), P("row", None))
    return jax.shard_map(
        local, mesh=mesh, in_specs=placed, out_specs=P("row", "col", None, None), check_vma=False
    )
```

```python
import math

import jax
import jax.numpy as jnp
from jax import lax
from jax.experimental import pallas as pl
from jax.experimental.pallas import tpu as pltpu
from jax.sharding import PartitionSpec as P

MESH = pl.DeviceIdType.MESH
HEADS = 12
HEAD = 128
GROUPS = 12
WIDE = 128
WINDOW = 2
ORDER = (0, 1, 2)
PAD = 80
INNER = 1536
D = 3072
CH = 512
SHARD = 864
HALF = 432
ROWS = 576
CHUNK = 512
F32 = jnp.float32
BF16 = jnp.bfloat16


def lanes(start, size):
    return pl.ds(pl.multiple_of(start, 128), size)


def body(q_ref, k_ref, v_ref, t_ref, wo_ref, wp_ref, cw_ref, out_ref,
         win, att, home, res, tok, wo, wp, cw, shard, field, acc, perm4, perm2, back, sent, mid, got, ssq,
         fs, fr, rs, rr, ls, ws, wr, hs, hr, os_, or_, cs, cr):
    r = lax.axis_index("row")
    c = lax.axis_index("col")
    odd = lax.rem(r, 2)
    x, zh = lax.div(c, 2), lax.rem(c, 2)
    y, zl = lax.div(r, 4), lax.rem(lax.div(r, 2), 2)

    def at(row, col):
        return (lax.rem(row + 16, 16), lax.rem(col + 8, 8))

    def along_x(step):
        return (r, lax.rem(x + step, 4) * 2 + zh)

    def along_y(step):
        return (lax.rem(y + step, 4) * 4 + zl * 2 + odd, c)

    other_zl = (y * 4 + (1 - zl) * 2 + odd, c)
    other_core = (r + 1 - 2 * odd, c)
    forward = (at(r - 1, c - odd), at(r - 1, c + 1 - odd), at(r, c - 1 + 2 * odd))
    homes = (at(r + 1, c + 1 - odd), at(r + 1, c - odd), at(r, c + 1 - 2 * odd))
    around = [(dr, dc) for dr in (-1, 0, 1) for dc in (-1, 0, 1) if (dr, dc) != (0, 0)]

    barrier = pltpu.get_barrier_semaphore()

    def greet(device):
        pl.semaphore_signal(barrier, inc=1, device_id=device, device_id_type=MESH)

    for step in range(1, 16):
        greet(at(r + step, c))
    for step in range(1, 8):
        greet(at(r, c + step))
    for dr, dc in ((-1, -1), (-1, 1), (1, -1), (1, 1)):
        greet(at(r + dr, c + dc))

    local = [
        pltpu.make_async_copy(cw_ref, shard, ls.at[0]),
        pltpu.make_async_copy(t_ref, tok, ls.at[1]),
        pltpu.make_async_copy(wo_ref, wo, ls.at[2]),
        pltpu.make_async_copy(wp_ref, wp, ls.at[3]),
    ]
    sources = (q_ref, k_ref, v_ref)
    for n in range(3):
        local.append(
            pltpu.make_async_copy(
                sources[n].at[pl.ds(3, 3), pl.ds(3 * (1 - odd), 3)], win.at[n, odd], ls.at[4 + n]
            )
        )
    local[0].start()
    for copy in local[4:]:
        copy.start()

    pl.semaphore_wait(barrier, 26)

    def send(g, n, t):
        span = lanes(g * WIDE, WIDE)
        if t == 2:
            src = sources[n].at[pl.ds(3, 3), pl.ds(3 * odd, 3), :, span]
            dst = win.at[n, 1 - odd, :, :, :, span]
        else:
            src = sources[n].at[pl.ds(0, 3), pl.ds(3 * t, 3), :, span]
            dst = win.at[n, 3 - t, :, :, :, span]
        return pltpu.make_async_remote_copy(
            src_ref=src, dst_ref=dst, send_sem=fs.at[g, n, t], recv_sem=fr.at[g, n, t],
            device_id=forward[t], device_id_type=MESH,
        )

    def give(g, t):
        span = lanes(g * WIDE, WIDE)
        if t == 2:
            src = att.at[1 - odd, :, :, :, span]
            dst = home.at[pl.ds(3, 3), pl.ds(3 * odd, 3), :, span]
        else:
            src = att.at[3 - t, :, :, :, span]
            dst = home.at[pl.ds(0, 3), pl.ds(3 * t, 3), :, span]
        return pltpu.make_async_remote_copy(
            src_ref=src, dst_ref=dst, send_sem=rs.at[g, t], recv_sem=rr.at[g, t],
            device_id=homes[t], device_id_type=MESH,
        )

    def keep(g):
        span = lanes(g * WIDE, WIDE)
        return pltpu.make_async_copy(
            att.at[odd, :, :, :, span], home.at[pl.ds(3, 3), pl.ds(3 * (1 - odd), 3), :, span], rr.at[g, 3]
        )

    def send_group(g):
        for n in range(3):
            for t in ORDER:
                send(g, n, t).start()

    for g in range(WINDOW):
        send_group(g)
    for copy in local[1:4]:
        copy.start()

    quarter = lanes(x * 128, 128)
    everything = pl.ds(0, CH)

    def piece(i, y_, zl_, part, span, device):
        first, size = part
        start = pl.multiple_of((y_ * 4 + zl_ * 2 + odd) * SHARD + first, 16)
        block = cw.at[pl.ds(start, size), span]
        return pltpu.make_async_remote_copy(
            src_ref=block, dst_ref=block, send_sem=ws.at[i], recv_sem=wr.at[i],
            device_id=device, device_id_type=MESH,
        )

    def whose_y(step):
        return lax.rem(y + step, 4)

    low, high, full = (0, HALF), (HALF, HALF), (0, SHARD)
    steps = (1, 3, 2)
    cross = [(0, y, zl, full, quarter, other_zl)]
    own_low = [(s, y, zl, low, quarter, along_y(s)) for s in steps]
    own_high = [(3 + s, y, zl, high, everything, along_y(s)) for s in steps]
    far_low = [(6 + s, y, 1 - zl, low, quarter, along_y(s)) for s in steps]
    far_high = [(9 + s, y, 1 - zl, high, quarter, along_x(s)) for s in steps]
    far_spread = [(12 + s, y, 1 - zl, low, quarter, along_x(s)) for s in steps]
    near = [[(12 + 3 * d + s, whose_y(d), zl, low, quarter, along_x(s)) for s in steps] for d in (1, 2, 3)]
    far_rows = [(24 + s, y, 1 - zl, high, everything, along_y(s)) for s in steps]
    far = [[(24 + 3 * d + s, whose_y(d), 1 - zl, low, quarter, along_x(s)) for s in steps] for d in (1, 2, 3)]
    swap_own = [(37, y, zl, full, everything, other_core)]
    swap_high = [(37 + d, whose_y(d), zl, high, everything, other_core) for d in (1, 2, 3)]
    swap_far = [(41, y, 1 - zl, full, everything, other_core)]
    swap_low = [(41 + d, whose_y(d), zl, low, everything, other_core) for d in (1, 2, 3)]
    swap_rest = [(44 + d, whose_y(d), 1 - zl, full, everything, other_core) for d in (1, 2, 3)]
    swaps = swap_own + swap_high + swap_far + swap_low + swap_rest
    before_groups = cross + own_low + swap_own
    plan = {
        0: ([], own_high[:1]),
        1: (cross, far_low + far_high + own_high[1:2]),
        2: (own_low, far_spread + near[0] + own_high[2:]),
        3: ([], near[1] + near[2]),
        4: (far_high, far_rows[:1]),
        5: (far_low, far_rows[1:2] + far[0]),
        6: ([], far_rows[2:] + far[1]),
        7: (own_high, far[2] + swap_high),
        8: (far_spread, swap_far),
        9: (near[0] + near[1] + near[2], swap_low),
        10: (far_rows + far[0] + far[1] + far[2], swap_rest),
    }
    pieces_sent = before_groups + [item for _, leaving in plan.values() for item in leaving]

    def start_all(pieces):
        for item in pieces:
            piece(*item).start()

    def wait_all(pieces):
        for item in pieces:
            piece(*item).wait_recv()

    def drain(pieces):
        for item in pieces:
            piece(*item).wait_send()

    local[0].wait()
    key = lax.broadcasted_iota(jnp.int32, (CH, CH), 0)
    lane = lax.broadcasted_iota(jnp.int32, (CH, CH), 1)
    order = jnp.where(key == 4 * (lane & 127) + (lane >> 7), 1.0, 0.0).astype(BF16)
    own_start = pl.multiple_of(r * SHARD, 16)
    for part in range(3):
        cw[pl.ds(own_start + 288 * part, 288), :] = jnp.dot(
            shard[pl.ds(288 * part, 288), :], order, preferred_element_type=F32
        ).astype(BF16)
    start_all(before_groups)

    def reorder(count, size):
        shape = (16 * size, count * 192)
        row = lax.broadcasted_iota(jnp.int32, shape, 0)
        col = lax.broadcasted_iota(jnp.int32, shape, 1)
        frame = row >> 4
        if size == 48:
            frame = (row * 21846) >> 20
        elif size == 32:
            frame = row >> 5
        place = row - frame * size
        strip = (place * 171) >> 11
        across = place - strip * 12
        wanted = (across & 1) * (count * 96) + strip * 96 + (across >> 1) * 16 + frame
        return jnp.where(jnp.logical_and(place < 12 * count, col == wanted), 1.0, 0.0).astype(BF16)

    perm4[...] = reorder(4, 48)
    perm2[...] = reorder(2, 32)
    row = lax.broadcasted_iota(jnp.int32, (ROWS, 8 * PAD), 0)
    col = lax.broadcasted_iota(jnp.int32, (ROWS, 8 * PAD), 1)
    strip = (row * 683) >> 16
    place = row - strip * 96
    which = (place * 171) >> 11
    wanted = which * PAD + strip * 12 + place - which * 12
    back[...] = jnp.where(col == wanted, 1.0, 0.0).astype(BF16)

    for copy in local[4:]:
        copy.wait()

    def attend(h):
        span = lanes(h * HEAD, HEAD)
        keys = win[1, :, :, :, :, span].reshape(ROWS, HEAD)
        values = win[2, :, :, :, :, span].reshape(ROWS, HEAD)
        for part in range(2):
            queries = win[0, pl.ds(2 * part, 2), :, :, :, span].reshape(ROWS // 2, HEAD)
            scores = lax.dot_general(
                queries, keys, (((1,), (1,)), ((), ())), preferred_element_type=F32
            ) * (1.0 / math.sqrt(HEAD))
            highest = jnp.max(scores, axis=-1, keepdims=True)
            weights = jnp.exp(scores - highest)
            probs = (weights * (1.0 / jnp.sum(weights, axis=-1, keepdims=True))).astype(BF16)
            mixed = jnp.dot(probs, values, preferred_element_type=F32).astype(BF16)
            att[pl.ds(2 * part, 2), :, :, :, span] = mixed.reshape(2, 3, 3, 16, HEAD)

    def await_home(g):
        for t in range(3):
            give(g, t).wait_recv()
        keep(g).wait()

    def add_pair(g, first):
        await_home(g)
        await_home(g + 1)
        rows = home[:, :, :, lanes(g * WIDE, 2 * WIDE)].reshape(ROWS, 2 * WIDE)

        def chunk(n, carry):
            span = lanes(n * CHUNK, CHUNK)
            product = jnp.dot(
                rows, wo[pl.ds(pl.multiple_of(g * WIDE, WIDE), 2 * WIDE), span], preferred_element_type=F32
            )
            base = tok[:, span].astype(F32) if first else res[:, span]
            res[:, span] = base + product
            return carry

        lax.fori_loop(0, D // CHUNK, chunk, 0)

    def group(g, carry):
        for n in range(3):
            for t in range(3):
                send(g, n, t).wait_recv()

        @pl.when(g < GROUPS - WINDOW)
        def _():
            for n in range(3):
                for t in range(3):
                    send(g, n, t).wait_send()
            send_group(g + WINDOW)

        for h in range(WIDE // HEAD):
            attend(g * (WIDE // HEAD) + h)
        for t in ORDER:
            give(g, t).start()
        keep(g).start()

        def weights_step(arriving, leaving):
            def _():
                wait_all(arriving)
                start_all(leaving)

            return _

        for at_group, (arriving, leaving) in plan.items():
            pl.when(g == at_group)(weights_step(arriving, leaving))

        @pl.when(g == 2)
        def _():
            for copy in local[1:4]:
                copy.wait()
            add_pair(0, True)

        @pl.when(jnp.logical_and(g > 2, lax.rem(g, 2) == 0))
        def _():
            add_pair(g - 2, False)

        return carry

    lax.fori_loop(0, GROUPS, group, 0)

    last = GROUPS - 2
    await_home(last)
    await_home(last + 1)
    rows = home[:, :, :, pl.ds(last * WIDE, 2 * WIDE)].reshape(ROWS, 2 * WIDE)
    ssq[...] = jnp.zeros_like(ssq)
    acc[...] = jnp.zeros_like(acc)

    def finish(n, carry):
        span = lanes(n * CHUNK, CHUNK)
        total = res[:, span] + jnp.dot(rows, wo[pl.ds(last * WIDE, 2 * WIDE), span], preferred_element_type=F32)
        ssq[...] += jnp.sum(total * total, axis=-1, keepdims=True)
        acc[...] += jnp.dot(
            total.astype(BF16), wp[pl.ds(pl.multiple_of(n * CHUNK, CHUNK), CHUNK), :], preferred_element_type=F32
        )
        return carry

    lax.fori_loop(0, D // CHUNK, finish, 0)
    raw = acc[...] * lax.rsqrt(ssq[...] * (1.0 / D) + 1e-6)
    features = (raw / (1.0 + jnp.exp(-raw))).astype(BF16)
    field[pl.ds(1, 6), pl.ds(1, 6)] = features.reshape(6, 6, 16, CH)

    def rim(i):
        dr, dc = around[i]
        take = [pl.ds(1, 6) if d == 0 else (1 if d < 0 else 6) for d in (dr, dc)]
        put = [pl.ds(1, 6) if d == 0 else (7 if d < 0 else 0) for d in (dr, dc)]
        return pltpu.make_async_remote_copy(
            src_ref=field.at[take[0], take[1]], dst_ref=field.at[put[0], put[1]],
            send_sem=hs.at[i], recv_sem=hr.at[i],
            device_id=at(r + dr, c + dc), device_id_type=MESH,
        )

    sides = (0, 2, 3, 4, 5, 7)
    for i in sides + (1, 6):
        rim(i).start()
    wait_all(swaps)
    for i in (1, 6):
        rim(i).wait()

    @pl.when(r == 0)
    def _():
        field[0, pl.ds(1, 6)] = jnp.zeros((6, 16, CH), BF16)

    @pl.when(r == 15)
    def _():
        field[7, pl.ds(1, 6)] = jnp.zeros((6, 16, CH), BF16)

    def tap_rows(dt, dy, dx):
        return pl.ds(pl.multiple_of(((dt * 3 + dy) * 3 + dx) * CH, CH), CH)

    def centre(step, carry):
        a, dt = lax.div(step, 3), lax.rem(step, 3)
        total = jnp.zeros((ROWS, 256), F32)
        for dy in range(3):
            total += jnp.dot(
                field[pl.ds(dy, 6), pl.ds(1, 6)].reshape(ROWS, CH), cw[tap_rows(dt, dy, 1), lanes(a * 256, 256)],
                preferred_element_type=F32,
            )
        res[:, lanes(step * 256, 256)] = total
        return carry

    lax.fori_loop(0, 6, centre, 0)

    for i in sides:
        rim(i).wait()

    @pl.when(r == 0)
    def _():
        field[0] = jnp.zeros((8, 16, CH), BF16)

    @pl.when(r == 15)
    def _():
        field[7] = jnp.zeros((8, 16, CH), BF16)

    @pl.when(c == 0)
    def _():
        field[:, 0] = jnp.zeros((8, 16, CH), BF16)

    @pl.when(c == 7)
    def _():
        field[:, 7] = jnp.zeros((8, 16, CH), BF16)

    def to_row(a, f):
        return pltpu.make_async_remote_copy(
            src_ref=sent.at[a, f], dst_ref=mid.at[a, r], send_sem=os_.at[a, f], recv_sem=or_.at[a, r],
            device_id=(f, c), device_id_type=MESH,
        )

    def row_arrival(a, i):
        return pltpu.make_async_remote_copy(
            src_ref=sent.at[a, i], dst_ref=mid.at[a, i], send_sem=os_.at[a, i], recv_sem=or_.at[a, i],
            device_id=(i, c), device_id_type=MESH,
        )

    def row_stay(a):
        return pltpu.make_async_copy(sent.at[a, r], mid.at[a, r], or_.at[a, r])

    def to_col(a, col):
        return pltpu.make_async_remote_copy(
            src_ref=mid.at[a, pl.ds(2 * col, 2)], dst_ref=got.at[a, :, c], send_sem=cs.at[a, col], recv_sem=cr.at[a, c],
            device_id=(r, col), device_id_type=MESH,
        )

    def col_arrival(a, i):
        return pltpu.make_async_remote_copy(
            src_ref=mid.at[a, pl.ds(0, 2)], dst_ref=got.at[a, :, i], send_sem=cs.at[a, i], recv_sem=cr.at[a, i],
            device_id=(r, i), device_id_type=MESH,
        )

    def col_stay(a):
        return pltpu.make_async_copy(mid.at[a, pl.ds(2 * c, 2)], got.at[a, :, c], cr.at[a, c])

    age = lax.broadcasted_iota(jnp.int32, (ROWS, 256), 0) & 15

    def convolve(a):
        def tap(dt, carry):
            spot = lanes((a * 3 + dt) * 256, 256)
            total = res[:, spot]
            for dy in range(3):
                for dx in (0, 2):
                    total += jnp.dot(
                        field[pl.ds(dy, 6), pl.ds(dx, 6)].reshape(ROWS, CH),
                        cw[tap_rows(dt, dy, dx), pl.ds(a * 256, 256)],
                        preferred_element_type=F32,
                    )
            res[:, spot] = total
            return carry

        lax.fori_loop(0, 3, tap, 0)
        first = a * 768
        conv = res[:, first + 512 : first + 768]
        conv += jnp.where(age >= 1, pltpu.roll(res[:, first + 256 : first + 512], 1, axis=0), 0.0)
        conv += jnp.where(age >= 2, pltpu.roll(res[:, first : first + 256], 2, axis=0), 0.0)
        done = conv.astype(BF16)
        for rows, table, start, size in ((done[:384], perm4, 0, 48), (done[384:], perm2, 48, 32)):
            stacked = jnp.concatenate([rows[:, :128], rows[:, 128:]], axis=0)
            moved = jnp.dot(table[...], stacked, preferred_element_type=F32).astype(BF16)
            sent[a, :, pl.ds(start, size), :] = moved.reshape(16, size, 128)

        row_stay(a).start()
        for step in range(1, 16):
            to_row(a, lax.rem(r + step, 16)).start()

    def pass_on(a):
        row_stay(a).wait()
        for step in range(1, 16):
            row_arrival(a, lax.rem(r + step, 16)).wait_recv()
        col_stay(a).start()
        for step in range(1, 8):
            to_col(a, lax.rem(c + step, 8)).start()

    def collect(a):
        col_stay(a).wait()
        for step in range(1, 8):
            col_arrival(a, lax.rem(c + step, 8)).wait_recv()
        for half in range(2):
            block = jnp.dot(
                back[...], got[a, half].reshape(8 * PAD, 128), preferred_element_type=F32
            ).astype(BF16)
            for i in range(6):
                out_ref[12 * half + 2 * i + a] = block[96 * i : 96 * i + 96]

    convolve(0)
    convolve(1)
    pass_on(0)
    pass_on(1)
    collect(0)
    collect(1)

    def drain_group(g, carry):
        @pl.when(g >= GROUPS - WINDOW)
        def _():
            for n in range(3):
                for t in range(3):
                    send(g, n, t).wait_send()

        for t in range(3):
            give(g, t).wait_send()
        return carry

    lax.fori_loop(0, GROUPS, drain_group, 0)
    drain(pieces_sent)

    for a in range(2):
        for step in range(1, 16):
            to_row(a, lax.rem(r + step, 16)).wait_send()
        for step in range(1, 8):
            to_col(a, lax.rem(c + step, 8)).wait_send()


def local(queries, keys, values, tokens, out_weight, proj_weight, conv_weight):
    cells = [jnp.transpose(a, (1, 2, 0, 3)) for a in (queries, keys, values)]
    rows = jnp.transpose(tokens, (1, 2, 0, 3)).reshape(ROWS, D)
    anywhere = pl.BlockSpec(memory_space=pl.ANY)
    dma = pltpu.SemaphoreType.DMA
    out = pl.pallas_call(
        body,
        out_shape=jax.ShapeDtypeStruct((24, 96, 128), BF16),
        in_specs=[anywhere] * 7,
        out_specs=pl.BlockSpec(memory_space=pltpu.VMEM),
        scratch_shapes=[
            pltpu.VMEM((3, 4, 3, 3, 16, INNER), BF16),
            pltpu.VMEM((4, 3, 3, 16, INNER), BF16),
            pltpu.VMEM((6, 6, 16, INNER), BF16),
            pltpu.VMEM((ROWS, D), F32),
            pltpu.VMEM((ROWS, D), BF16),
            pltpu.VMEM((INNER, D), BF16),
            pltpu.VMEM((D, CH), BF16),
            pltpu.VMEM((16 * SHARD, CH), BF16),
            pltpu.VMEM((SHARD, CH), BF16),
            pltpu.VMEM((8, 8, 16, CH), BF16),
            pltpu.VMEM((ROWS, CH), F32),
            pltpu.VMEM((768, 768), BF16),
            pltpu.VMEM((512, 384), BF16),
            pltpu.VMEM((ROWS, 8 * PAD), BF16),
            pltpu.VMEM((2, 16, PAD, 128), BF16),
            pltpu.VMEM((2, 16, PAD, 128), BF16),
            pltpu.VMEM((2, 2, 8, PAD, 128), BF16),
            pltpu.VMEM((ROWS, 1), F32),
            dma((GROUPS, 3, 3)), dma((GROUPS, 3, 3)),
            dma((GROUPS, 3)), dma((GROUPS, 4)),
            dma((7,)),
            dma((48,)), dma((48,)),
            dma((8,)), dma((8,)),
            dma((2, 16)), dma((2, 16)),
            dma((2, 8)), dma((2, 8)),
        ],
        compiler_params=pltpu.CompilerParams(
            collective_id=0, has_side_effects=True, vmem_limit_bytes=62 * 1024 * 1024
        ),
    )(*cells, rows, out_weight, proj_weight, conv_weight)
    return out[None]


def solution(mesh):
    tile = P(None, "row", "col", None)
    placed = (tile, tile, tile, tile, P(), P(), P("row", None))
    return jax.shard_map(
        local, mesh=mesh, in_specs=placed, out_specs=P("row", "col", None, None), check_vma=False
    )
```

```python
import math

import jax
import jax.numpy as jnp
from jax import lax
from jax.experimental import pallas as pl
from jax.experimental.pallas import tpu as pltpu
from jax.sharding import PartitionSpec as P

MESH = pl.DeviceIdType.MESH
HEADS = 12
HEAD = 128
GROUPS = 12
WIDE = 128
WINDOW = 2
ORDER = (0, 1, 2)
PAD = 80
INNER = 1536
D = 3072
CH = 512
SHARD = 864
HALF = 432
ROWS = 576
CHUNK = 512
F32 = jnp.float32
BF16 = jnp.bfloat16


def lanes(start, size):
    return pl.ds(pl.multiple_of(start, 128), size)


def body(q_ref, k_ref, v_ref, t_ref, wo_ref, wp_ref, cw_ref, out_ref,
         win, att, home, res, tok, wo, wp, cw, shard, field, acc, perm4, perm2, back, sent, mid, got, both,
         fs, fr, rs, rr, ls, ws, wr, hs, hr, os_, or_, cs, cr):
    r = lax.axis_index("row")
    c = lax.axis_index("col")
    odd = lax.rem(r, 2)
    x, zh = lax.div(c, 2), lax.rem(c, 2)
    y, zl = lax.div(r, 4), lax.rem(lax.div(r, 2), 2)

    def at(row, col):
        return (lax.rem(row + 16, 16), lax.rem(col + 8, 8))

    def along_x(step):
        return (r, lax.rem(x + step, 4) * 2 + zh)

    def along_y(step):
        return (lax.rem(y + step, 4) * 4 + zl * 2 + odd, c)

    other_zl = (y * 4 + (1 - zl) * 2 + odd, c)
    other_core = (r + 1 - 2 * odd, c)
    forward = (at(r - 1, c - odd), at(r - 1, c + 1 - odd), at(r, c - 1 + 2 * odd))
    homes = (at(r + 1, c + 1 - odd), at(r + 1, c - odd), at(r, c + 1 - 2 * odd))
    around = [(dr, dc) for dr in (-1, 0, 1) for dc in (-1, 0, 1) if (dr, dc) != (0, 0)]

    barrier = pltpu.get_barrier_semaphore()

    def greet(device):
        pl.semaphore_signal(barrier, inc=1, device_id=device, device_id_type=MESH)

    for dr, dc in around:
        greet(at(r + dr, c + dc))
    for step in (1, 2, 3):
        greet(along_x(step))
        greet(along_y(step))
    greet(other_zl)
    greet(other_core)
    own_corner = zl == zh
    for half in range(2):
        for col in range(8):
            row = 4 * y + 2 * zh + half

            @pl.when(jnp.logical_or(row != r, col != c))
            def _(row=row, col=col):
                greet((row, col))

    local = [
        pltpu.make_async_copy(cw_ref, shard, ls.at[0]),
        pltpu.make_async_copy(t_ref, tok, ls.at[1]),
        pltpu.make_async_copy(wo_ref, wo, ls.at[2]),
        pltpu.make_async_copy(wp_ref, wp, ls.at[3]),
    ]
    sources = (q_ref, k_ref, v_ref)
    for n in range(3):
        local.append(
            pltpu.make_async_copy(
                sources[n].at[pl.ds(3, 3), pl.ds(3 * (1 - odd), 3)], win.at[n, odd], ls.at[4 + n]
            )
        )
    local[0].start()
    for copy in local[4:]:
        copy.start()

    pl.semaphore_wait(barrier, 32 - own_corner.astype(jnp.int32))

    def send(g, n, t):
        span = lanes(g * WIDE, WIDE)
        if t == 2:
            src = sources[n].at[pl.ds(3, 3), pl.ds(3 * odd, 3), :, span]
            dst = win.at[n, 1 - odd, :, :, :, span]
        else:
            src = sources[n].at[pl.ds(0, 3), pl.ds(3 * t, 3), :, span]
            dst = win.at[n, 3 - t, :, :, :, span]
        return pltpu.make_async_remote_copy(
            src_ref=src, dst_ref=dst, send_sem=fs.at[g, n, t], recv_sem=fr.at[g, n, t],
            device_id=forward[t], device_id_type=MESH,
        )

    def give(g, t):
        span = lanes(g * WIDE, WIDE)
        if t == 2:
            src = att.at[1 - odd, :, :, :, span]
            dst = home.at[pl.ds(3, 3), pl.ds(3 * odd, 3), :, span]
        else:
            src = att.at[3 - t, :, :, :, span]
            dst = home.at[pl.ds(0, 3), pl.ds(3 * t, 3), :, span]
        return pltpu.make_async_remote_copy(
            src_ref=src, dst_ref=dst, send_sem=rs.at[g, t], recv_sem=rr.at[g, t],
            device_id=homes[t], device_id_type=MESH,
        )

    def keep(g):
        span = lanes(g * WIDE, WIDE)
        return pltpu.make_async_copy(
            att.at[odd, :, :, :, span], home.at[pl.ds(3, 3), pl.ds(3 * (1 - odd), 3), :, span], rr.at[g, 3]
        )

    def send_group(g):
        for n in range(3):
            for t in ORDER:
                send(g, n, t).start()

    for g in range(WINDOW):
        send_group(g)
    for copy in local[1:4]:
        copy.start()

    quarter = lanes(x * 128, 128)
    everything = pl.ds(0, CH)

    def piece(i, y_, zl_, part, span, device):
        first, size = part
        start = pl.multiple_of((y_ * 4 + zl_ * 2 + odd) * SHARD + first, 16)
        block = cw.at[pl.ds(start, size), span]
        return pltpu.make_async_remote_copy(
            src_ref=block, dst_ref=block, send_sem=ws.at[i], recv_sem=wr.at[i],
            device_id=device, device_id_type=MESH,
        )

    def whose_y(step):
        return lax.rem(y + step, 4)

    low, high, full = (0, HALF), (HALF, HALF), (0, SHARD)
    steps = (1, 3, 2)
    cross = [(0, y, zl, full, quarter, other_zl)]
    own_low = [(s, y, zl, low, quarter, along_y(s)) for s in steps]
    own_high = [(3 + s, y, zl, high, everything, along_y(s)) for s in steps]
    far_low = [(6 + s, y, 1 - zl, low, quarter, along_y(s)) for s in steps]
    far_high = [(9 + s, y, 1 - zl, high, quarter, along_x(s)) for s in steps]
    far_spread = [(12 + s, y, 1 - zl, low, quarter, along_x(s)) for s in steps]
    near = [[(12 + 3 * d + s, whose_y(d), zl, low, quarter, along_x(s)) for s in steps] for d in (1, 2, 3)]
    far_rows = [(24 + s, y, 1 - zl, high, everything, along_y(s)) for s in steps]
    far = [[(24 + 3 * d + s, whose_y(d), 1 - zl, low, quarter, along_x(s)) for s in steps] for d in (1, 2, 3)]
    swap_own = [(37, y, zl, full, everything, other_core)]
    swap_high = [(37 + d, whose_y(d), zl, high, everything, other_core) for d in (1, 2, 3)]
    swap_far = [(41, y, 1 - zl, full, everything, other_core)]
    swap_low = [(41 + d, whose_y(d), zl, low, everything, other_core) for d in (1, 2, 3)]
    swap_rest = [(44 + d, whose_y(d), 1 - zl, full, everything, other_core) for d in (1, 2, 3)]
    swaps = swap_own + swap_high + swap_far + swap_low + swap_rest
    before_groups = cross + own_low + swap_own
    plan = {
        0: ([], own_high[:1]),
        1: (cross, far_low + far_high + own_high[1:2]),
        2: (own_low, far_spread + near[0] + own_high[2:]),
        3: ([], near[1] + near[2]),
        4: (far_high, far_rows[:1]),
        5: (far_low, far_rows[1:2] + far[0]),
        6: ([], far_rows[2:] + far[1]),
        7: (own_high, far[2] + swap_high),
        8: (far_spread, swap_far),
        9: (near[0] + near[1] + near[2], swap_low),
        10: (far_rows + far[0] + far[1] + far[2], swap_rest),
    }
    pieces_sent = before_groups + [item for _, leaving in plan.values() for item in leaving]

    def start_all(pieces):
        for item in pieces:
            piece(*item).start()

    def wait_all(pieces):
        for item in pieces:
            piece(*item).wait_recv()

    def drain(pieces):
        for item in pieces:
            piece(*item).wait_send()

    local[0].wait()
    key = lax.broadcasted_iota(jnp.int32, (CH, CH), 0)
    lane = lax.broadcasted_iota(jnp.int32, (CH, CH), 1)
    order = jnp.where(key == 4 * (lane & 127) + (lane >> 7), 1.0, 0.0).astype(BF16)
    own_start = pl.multiple_of(r * SHARD, 16)
    for part in range(3):
        cw[pl.ds(own_start + 288 * part, 288), :] = jnp.dot(
            shard[pl.ds(288 * part, 288), :], order, preferred_element_type=F32
        ).astype(BF16)
    start_all(before_groups)

    def reorder(count, size):
        shape = (16 * size, count * 192)
        row = lax.broadcasted_iota(jnp.int32, shape, 0)
        col = lax.broadcasted_iota(jnp.int32, shape, 1)
        frame = row >> 4
        if size == 48:
            frame = (row * 21846) >> 20
        elif size == 32:
            frame = row >> 5
        place = row - frame * size
        strip = (place * 171) >> 11
        across = place - strip * 12
        wanted = (across & 1) * (count * 96) + strip * 96 + (across >> 1) * 16 + frame
        return jnp.where(jnp.logical_and(place < 12 * count, col == wanted), 1.0, 0.0).astype(BF16)

    perm4[...] = reorder(4, 48)
    perm2[...] = reorder(2, 32)
    row = lax.broadcasted_iota(jnp.int32, (ROWS, 8 * PAD), 0)
    col = lax.broadcasted_iota(jnp.int32, (ROWS, 8 * PAD), 1)
    strip = (row * 683) >> 16
    place = row - strip * 96
    which = (place * 171) >> 11
    wanted = which * PAD + strip * 12 + place - which * 12
    back[...] = jnp.where(col == wanted, 1.0, 0.0).astype(BF16)

    for copy in local[4:]:
        copy.wait()

    def attend(h):
        span = lanes(h * HEAD, HEAD)
        keys = win[1, :, :, :, :, span].reshape(ROWS, HEAD)
        values = win[2, :, :, :, :, span].reshape(ROWS, HEAD)
        for part in range(2):
            queries = win[0, pl.ds(2 * part, 2), :, :, :, span].reshape(ROWS // 2, HEAD)
            scores = lax.dot_general(
                queries, keys, (((1,), (1,)), ((), ())), preferred_element_type=F32
            ) * (1.0 / math.sqrt(HEAD))
            highest = jnp.max(scores, axis=-1, keepdims=True)
            weights = jnp.exp(scores - highest)
            probs = (weights * (1.0 / jnp.sum(weights, axis=-1, keepdims=True))).astype(BF16)
            mixed = jnp.dot(probs, values, preferred_element_type=F32).astype(BF16)
            att[pl.ds(2 * part, 2), :, :, :, span] = mixed.reshape(2, 3, 3, 16, HEAD)

    def await_home(g):
        for t in range(3):
            give(g, t).wait_recv()
        keep(g).wait()

    def add_pair(g, first):
        await_home(g)
        await_home(g + 1)
        rows = home[:, :, :, lanes(g * WIDE, 2 * WIDE)].reshape(ROWS, 2 * WIDE)

        def chunk(n, carry):
            span = lanes(n * CHUNK, CHUNK)
            product = jnp.dot(
                rows, wo[pl.ds(pl.multiple_of(g * WIDE, WIDE), 2 * WIDE), span], preferred_element_type=F32
            )
            base = tok[:, span].astype(F32) if first else res[:, :, :, span].reshape(ROWS, CHUNK)
            res[:, :, :, span] = (base + product).reshape(6, 6, 16, CHUNK)
            return carry

        lax.fori_loop(0, D // CHUNK, chunk, 0)

    last = GROUPS - 2

    def merge():
        both[...] = jnp.dot(
            wo[pl.ds(last * WIDE, 2 * WIDE), :], wp[...], preferred_element_type=F32
        ).astype(BF16)

    def project():
        acc[...] = jnp.zeros_like(acc)

        def chunk(n, carry):
            rows = pl.ds(pl.multiple_of(n * CHUNK, CHUNK), CHUNK)
            known = res[:, :, :, lanes(n * CHUNK, CHUNK)].reshape(ROWS, CHUNK).astype(BF16)
            acc[...] += jnp.dot(known, wp[rows, :], preferred_element_type=F32).reshape(6, 6, 16, CH)
            return carry

        lax.fori_loop(0, D // CHUNK, chunk, 0)

    def group(g, carry):
        @pl.when(g < GROUPS - WINDOW)
        def _():
            for n in range(3):
                for t in range(3):
                    send(g, n, t).wait_send()
            send_group(g + WINDOW)

        @pl.when(g == 3)
        def _():
            for copy in local[1:4]:
                copy.wait()
            add_pair(0, True)

        @pl.when(jnp.logical_and(g > 3, lax.rem(g, 2) == 1))
        def _():
            add_pair(g - 3, False)

        @pl.when(g == GROUPS - 2)
        def _():
            merge()

        @pl.when(g == GROUPS - 1)
        def _():
            project()

        for n in range(3):
            for t in range(3):
                send(g, n, t).wait_recv()

        for h in range(WIDE // HEAD):
            attend(g * (WIDE // HEAD) + h)
        for t in ORDER:
            give(g, t).start()
        keep(g).start()

        def weights_step(arriving, leaving):
            def _():
                wait_all(arriving)
                start_all(leaving)

            return _

        for at_group, (arriving, leaving) in plan.items():
            pl.when(g == at_group)(weights_step(arriving, leaving))

        return carry

    lax.fori_loop(0, GROUPS, group, 0)

    await_home(last)
    await_home(last + 1)
    def rim(i):
        dr, dc = around[i]
        take = [pl.ds(1, 6) if d == 0 else (1 if d < 0 else 6) for d in (dr, dc)]
        put = [pl.ds(1, 6) if d == 0 else (7 if d < 0 else 0) for d in (dr, dc)]
        return pltpu.make_async_remote_copy(
            src_ref=field.at[take[0], take[1]], dst_ref=field.at[put[0], put[1]],
            send_sem=hs.at[i], recv_sem=hr.at[i],
            device_id=at(r + dr, c + dc), device_id_type=MESH,
        )

    def columns(ref, spans, span):
        blocks = [ref[:, pl.ds(j, n), :, span] for j, n in spans]
        blocks = [block.reshape(-1, block.shape[-1]) for block in blocks]
        return blocks[0] if len(blocks) == 1 else jnp.concatenate(blocks, axis=0)

    def finish(spans):
        count = 96 * sum(n for _, n in spans)
        rows = columns(home, spans, pl.ds(last * WIDE, 2 * WIDE))

        def chunk(n, squares):
            span = lanes(n * CHUNK, CHUNK)
            total = columns(res, spans, span) + jnp.dot(
                rows, wo[pl.ds(last * WIDE, 2 * WIDE), span], preferred_element_type=F32
            )
            return squares + jnp.sum(total * total, axis=-1, keepdims=True)

        squares = lax.fori_loop(0, D // CHUNK, chunk, jnp.zeros((count, 1), F32))
        raw = columns(acc, spans, pl.ds(0, CH)) + jnp.dot(rows, both[...], preferred_element_type=F32)
        raw = raw * lax.rsqrt(squares * (1.0 / D) + 1e-6)
        features = (raw / (1.0 + jnp.exp(-raw))).astype(BF16)
        start = 0
        for j, n in spans:
            field[pl.ds(1, 6), pl.ds(1 + j, n)] = features[start : start + 96 * n].reshape(6, n, 16, CH)
            start += 96 * n

    sides = (0, 2, 3, 4, 5, 7)
    finish(((0, 1), (5, 1)))
    for i in sides:
        rim(i).start()
    finish(((1, 4),))
    for i in (1, 6):
        rim(i).start()
    wait_all(swaps)
    for i in (1, 6):
        rim(i).wait()

    @pl.when(r == 0)
    def _():
        field[0, pl.ds(1, 6)] = jnp.zeros((6, 16, CH), BF16)

    @pl.when(r == 15)
    def _():
        field[7, pl.ds(1, 6)] = jnp.zeros((6, 16, CH), BF16)

    def tap_rows(dt, dy, dx):
        return pl.ds(pl.multiple_of(((dt * 3 + dy) * 3 + dx) * CH, CH), CH)

    def centre(dt, carry):
        total = jnp.zeros((ROWS, CH), F32)
        for dy in range(3):
            total += jnp.dot(
                field[pl.ds(dy, 6), pl.ds(1, 6)].reshape(ROWS, CH), cw[tap_rows(dt, dy, 1), :],
                preferred_element_type=F32,
            )
        res[:, :, :, lanes(dt * 256, 256)] = total[:, :256].reshape(6, 6, 16, 256)
        res[:, :, :, lanes((dt + 3) * 256, 256)] = total[:, 256:].reshape(6, 6, 16, 256)
        return carry

    lax.fori_loop(0, 3, centre, 0)

    for i in sides:
        rim(i).wait()

    @pl.when(r == 0)
    def _():
        field[0] = jnp.zeros((8, 16, CH), BF16)

    @pl.when(r == 15)
    def _():
        field[7] = jnp.zeros((8, 16, CH), BF16)

    @pl.when(c == 0)
    def _():
        field[:, 0] = jnp.zeros((8, 16, CH), BF16)

    @pl.when(c == 7)
    def _():
        field[:, 7] = jnp.zeros((8, 16, CH), BF16)

    def to_y(a, step):
        there = whose_y(step)
        return pltpu.make_async_remote_copy(
            src_ref=sent.at[a, pl.ds(4 * there, 4)], dst_ref=mid.at[a, y],
            send_sem=os_.at[a, step], recv_sem=or_.at[a, step], device_id=along_y(step), device_id_type=MESH,
        )

    def hop(a, step, e):
        origin = whose_y(step)
        block = sent.at[a, 4 * y + e] if step == 0 else mid.at[a, origin, e]
        return origin, block

    def mine(origin, e):
        return jnp.logical_and(own_corner, jnp.logical_and(origin == x, e == 2 * zl + odd))

    def to_owner(a, step, e):
        origin, block = hop(a, step, e)
        return pltpu.make_async_remote_copy(
            src_ref=block, dst_ref=got.at[a, odd, c], send_sem=cs.at[a, 4 * step + e], recv_sem=cr.at[a, odd, c],
            device_id=(4 * y + e, 2 * origin + zl), device_id_type=MESH,
        )

    def own(a, step, e):
        _, block = hop(a, step, e)
        return pltpu.make_async_copy(block, got.at[a, odd, c], cr.at[a, odd, c])

    def arrival(a, half, col):
        return pltpu.make_async_remote_copy(
            src_ref=sent.at[a, 0], dst_ref=got.at[a, half, col], send_sem=cs.at[a, 0], recv_sem=cr.at[a, half, col],
            device_id=other_core, device_id_type=MESH,
        )

    def spread(a, step):
        for e in range(4):
            @pl.when(mine(whose_y(step), e))
            def _(e=e):
                own(a, step, e).start()

            @pl.when(jnp.logical_not(mine(whose_y(step), e)))
            def _(e=e):
                to_owner(a, step, e).start()

    age = lax.broadcasted_iota(jnp.int32, (ROWS, 256), 0) & 15

    def convolve(a):
        def tap(dt, carry):
            spot = lanes((a * 3 + dt) * 256, 256)
            total = res[:, :, :, spot].reshape(ROWS, 256)
            for dy in range(3):
                for dx in (0, 2):
                    total += jnp.dot(
                        field[pl.ds(dy, 6), pl.ds(dx, 6)].reshape(ROWS, CH),
                        cw[tap_rows(dt, dy, dx), pl.ds(a * 256, 256)],
                        preferred_element_type=F32,
                    )
            res[:, :, :, spot] = total.reshape(6, 6, 16, 256)
            return carry

        lax.fori_loop(0, 3, tap, 0)
        taps = [res[:, :, :, pl.ds((a * 3 + dt) * 256, 256)].reshape(ROWS, 256) for dt in range(3)]
        conv = taps[2]
        conv += jnp.where(age >= 1, pltpu.roll(taps[1], 1, axis=0), 0.0)
        conv += jnp.where(age >= 2, pltpu.roll(taps[0], 2, axis=0), 0.0)
        done = conv.astype(BF16)
        for rows, table, start, size in ((done[:384], perm4, 0, 48), (done[384:], perm2, 48, 32)):
            stacked = jnp.concatenate([rows[:, :128], rows[:, 128:]], axis=0)
            moved = jnp.dot(table[...], stacked, preferred_element_type=F32).astype(BF16)
            sent[a, :, pl.ds(start, size), :] = moved.reshape(16, size, 128)

        for step in (2, 1, 3):
            to_y(a, step).start()
        spread(a, 0)

    def pass_on(a):
        for step in (1, 3, 2):
            to_y(a, 4 - step).wait_recv()
            spread(a, step)

    def collect(a):
        for half in range(2):
            for col in range(8):
                arrival(a, half, col).wait_recv()
        for half in range(2):
            block = jnp.dot(
                back[...], got[a, half].reshape(8 * PAD, 128), preferred_element_type=F32
            ).astype(BF16)
            for i in range(6):
                out_ref[12 * half + 2 * i + a] = block[96 * i : 96 * i + 96]

    convolve(0)
    convolve(1)
    pass_on(0)
    pass_on(1)
    collect(0)
    collect(1)

    def drain_group(g, carry):
        @pl.when(g >= GROUPS - WINDOW)
        def _():
            for n in range(3):
                for t in range(3):
                    send(g, n, t).wait_send()

        for t in range(3):
            give(g, t).wait_send()
        return carry

    lax.fori_loop(0, GROUPS, drain_group, 0)
    drain(pieces_sent)

    for a in range(2):
        for step in range(4):
            if step:
                to_y(a, step).wait_send()
            for e in range(4):
                @pl.when(jnp.logical_not(mine(whose_y(step), e)))
                def _(a=a, step=step, e=e):
                    to_owner(a, step, e).wait_send()


def local(queries, keys, values, tokens, out_weight, proj_weight, conv_weight):
    cells = [jnp.transpose(a, (1, 2, 0, 3)) for a in (queries, keys, values)]
    rows = jnp.transpose(tokens, (1, 2, 0, 3)).reshape(ROWS, D)
    anywhere = pl.BlockSpec(memory_space=pl.ANY)
    dma = pltpu.SemaphoreType.DMA
    out = pl.pallas_call(
        body,
        out_shape=jax.ShapeDtypeStruct((24, 96, 128), BF16),
        in_specs=[anywhere] * 7,
        out_specs=pl.BlockSpec(memory_space=pltpu.VMEM),
        scratch_shapes=[
            pltpu.VMEM((3, 4, 3, 3, 16, INNER), BF16),
            pltpu.VMEM((4, 3, 3, 16, INNER), BF16),
            pltpu.VMEM((6, 6, 16, INNER), BF16),
            pltpu.VMEM((6, 6, 16, D), F32),
            pltpu.VMEM((ROWS, D), BF16),
            pltpu.VMEM((INNER, D), BF16),
            pltpu.VMEM((D, CH), BF16),
            pltpu.VMEM((16 * SHARD, CH), BF16),
            pltpu.VMEM((SHARD, CH), BF16),
            pltpu.VMEM((8, 8, 16, CH), BF16),
            pltpu.VMEM((6, 6, 16, CH), F32),
            pltpu.VMEM((768, 768), BF16),
            pltpu.VMEM((512, 384), BF16),
            pltpu.VMEM((ROWS, 8 * PAD), BF16),
            pltpu.VMEM((2, 16, PAD, 128), BF16),
            pltpu.VMEM((2, 4, 4, PAD, 128), BF16),
            pltpu.VMEM((2, 2, 8, PAD, 128), BF16),
            pltpu.VMEM((2 * WIDE, CH), BF16),
            dma((GROUPS, 3, 3)), dma((GROUPS, 3, 3)),
            dma((GROUPS, 3)), dma((GROUPS, 4)),
            dma((7,)),
            dma((48,)), dma((48,)),
            dma((8,)), dma((8,)),
            dma((2, 4)), dma((2, 4)),
            dma((2, 16)), dma((2, 2, 8)),
        ],
        compiler_params=pltpu.CompilerParams(
            collective_id=0, has_side_effects=True, vmem_limit_bytes=62 * 1024 * 1024
        ),
    )(*cells, rows, out_weight, proj_weight, conv_weight)
    return out[None]


def solution(mesh):
    tile = P(None, "row", "col", None)
    placed = (tile, tile, tile, tile, P(), P(), P("row", None))
    return jax.shard_map(
        local, mesh=mesh, in_specs=placed, out_specs=P("row", "col", None, None), check_vma=False
    )
```

```python
import math

import jax
import jax.numpy as jnp
from jax import lax
from jax.experimental import pallas as pl
from jax.experimental.pallas import tpu as pltpu
from jax.sharding import PartitionSpec as P

MESH = pl.DeviceIdType.MESH
HEADS = 12
HEAD = 128
GROUPS = 12
WIDE = 128
WINDOW = 2
ORDER = (0, 1, 2)
PAD = 80
INNER = 1536
D = 3072
CH = 512
SHARD = 864
HALF = 432
ROWS = 576
CHUNK = 512
F32 = jnp.float32
BF16 = jnp.bfloat16


def lanes(start, size):
    return pl.ds(pl.multiple_of(start, 128), size)


def body(q_ref, k_ref, v_ref, t_ref, wo_ref, wp_ref, cw_ref, out_ref,
         win, att, home, res, tok, wo, wp, cw, shard, field, side, acc, perm4, perm2, back, sent, mid, got, both,
         fs, fr, rs, rr, ls, ws, wr, hs, hr, os_, or_, cs, cr):
    r = lax.axis_index("row")
    c = lax.axis_index("col")
    odd = lax.rem(r, 2)
    x, zh = lax.div(c, 2), lax.rem(c, 2)
    y, zl = lax.div(r, 4), lax.rem(lax.div(r, 2), 2)

    def at(row, col):
        return (lax.rem(row + 16, 16), lax.rem(col + 8, 8))

    def along_x(step):
        return (r, lax.rem(x + step, 4) * 2 + zh)

    def along_y(step):
        return (lax.rem(y + step, 4) * 4 + zl * 2 + odd, c)

    other_zl = (y * 4 + (1 - zl) * 2 + odd, c)
    other_core = (r + 1 - 2 * odd, c)
    forward = (at(r - 1, c - odd), at(r - 1, c + 1 - odd), at(r, c - 1 + 2 * odd))
    homes = (at(r + 1, c + 1 - odd), at(r + 1, c - odd), at(r, c + 1 - 2 * odd))
    around = [(dr, dc) for dr in (-1, 0, 1) for dc in (-1, 0, 1) if (dr, dc) != (0, 0)]

    barrier = pltpu.get_barrier_semaphore()

    def greet(device):
        pl.semaphore_signal(barrier, inc=1, device_id=device, device_id_type=MESH)

    for dr, dc in around:
        greet(at(r + dr, c + dc))
    for step in (1, 2, 3):
        greet(along_x(step))
        greet(along_y(step))
    greet(other_zl)
    greet(other_core)
    own_corner = zl == zh
    for half in range(2):
        for col in range(8):
            row = 4 * y + 2 * zh + half

            @pl.when(jnp.logical_or(row != r, col != c))
            def _(row=row, col=col):
                greet((row, col))

    local = [
        pltpu.make_async_copy(cw_ref, shard, ls.at[0]),
        pltpu.make_async_copy(t_ref, tok, ls.at[1]),
        pltpu.make_async_copy(wo_ref, wo, ls.at[2]),
        pltpu.make_async_copy(wp_ref, wp, ls.at[3]),
    ]
    sources = (q_ref, k_ref, v_ref)
    for n in range(3):
        local.append(
            pltpu.make_async_copy(
                sources[n].at[pl.ds(3, 3), pl.ds(3 * (1 - odd), 3)], win.at[n, odd], ls.at[4 + n]
            )
        )
    local[0].start()
    for copy in local[4:]:
        copy.start()
    for j in (0, 7):
        field[:, j] = jnp.zeros((8, 16, CH), BF16)

    pl.semaphore_wait(barrier, 32 - own_corner.astype(jnp.int32))

    def send(g, n, t):
        span = lanes(g * WIDE, WIDE)
        if t == 2:
            src = sources[n].at[pl.ds(3, 3), pl.ds(3 * odd, 3), :, span]
            dst = win.at[n, 1 - odd, :, :, :, span]
        else:
            src = sources[n].at[pl.ds(0, 3), pl.ds(3 * t, 3), :, span]
            dst = win.at[n, 3 - t, :, :, :, span]
        return pltpu.make_async_remote_copy(
            src_ref=src, dst_ref=dst, send_sem=fs.at[g, n, t], recv_sem=fr.at[g, n, t],
            device_id=forward[t], device_id_type=MESH,
        )

    def give(g, t):
        span = lanes(g * WIDE, WIDE)
        if t == 2:
            src = att.at[1 - odd, :, :, :, span]
            dst = home.at[pl.ds(3, 3), pl.ds(3 * odd, 3), :, span]
        else:
            src = att.at[3 - t, :, :, :, span]
            dst = home.at[pl.ds(0, 3), pl.ds(3 * t, 3), :, span]
        return pltpu.make_async_remote_copy(
            src_ref=src, dst_ref=dst, send_sem=rs.at[g, t], recv_sem=rr.at[g, t],
            device_id=homes[t], device_id_type=MESH,
        )

    def keep(g):
        span = lanes(g * WIDE, WIDE)
        return pltpu.make_async_copy(
            att.at[odd, :, :, :, span], home.at[pl.ds(3, 3), pl.ds(3 * (1 - odd), 3), :, span], rr.at[g, 3]
        )

    def send_group(g):
        for n in range(3):
            for t in ORDER:
                send(g, n, t).start()

    for g in range(WINDOW):
        send_group(g)
    for copy in local[1:4]:
        copy.start()

    quarter = lanes(x * 128, 128)
    everything = pl.ds(0, CH)

    def piece(i, y_, zl_, part, span, device):
        first, size = part
        start = pl.multiple_of((y_ * 4 + zl_ * 2 + odd) * SHARD + first, 16)
        block = cw.at[pl.ds(start, size), span]
        return pltpu.make_async_remote_copy(
            src_ref=block, dst_ref=block, send_sem=ws.at[i], recv_sem=wr.at[i],
            device_id=device, device_id_type=MESH,
        )

    def whose_y(step):
        return lax.rem(y + step, 4)

    low, high, full = (0, HALF), (HALF, HALF), (0, SHARD)
    steps = (1, 3, 2)
    cross = [(0, y, zl, full, quarter, other_zl)]
    own_low = [(s, y, zl, low, quarter, along_y(s)) for s in steps]
    own_high = [(3 + s, y, zl, high, everything, along_y(s)) for s in steps]
    far_low = [(6 + s, y, 1 - zl, low, quarter, along_y(s)) for s in steps]
    far_high = [(9 + s, y, 1 - zl, high, quarter, along_x(s)) for s in steps]
    far_spread = [(12 + s, y, 1 - zl, low, quarter, along_x(s)) for s in steps]
    near = [[(12 + 3 * d + s, whose_y(d), zl, low, quarter, along_x(s)) for s in steps] for d in (1, 2, 3)]
    far_rows = [(24 + s, y, 1 - zl, high, everything, along_y(s)) for s in steps]
    far = [[(24 + 3 * d + s, whose_y(d), 1 - zl, low, quarter, along_x(s)) for s in steps] for d in (1, 2, 3)]
    swap_own = [(37, y, zl, full, everything, other_core)]
    swap_high = [(37 + d, whose_y(d), zl, high, everything, other_core) for d in (1, 2, 3)]
    swap_far = [(41, y, 1 - zl, full, everything, other_core)]
    swap_low = [(41 + d, whose_y(d), zl, low, everything, other_core) for d in (1, 2, 3)]
    swap_rest = [(44 + d, whose_y(d), 1 - zl, full, everything, other_core) for d in (1, 2, 3)]
    swaps = swap_own + swap_high + swap_far + swap_low + swap_rest
    before_groups = cross + own_low + swap_own
    plan = {
        0: ([], own_high[:1]),
        1: (cross, far_low + far_high + own_high[1:2]),
        2: (own_low, far_spread + near[0] + own_high[2:]),
        3: ([], near[1] + near[2]),
        4: (far_high, far_rows[:1]),
        5: (far_low, far_rows[1:2] + far[0]),
        6: ([], far_rows[2:] + far[1]),
        7: (own_high, far[2] + swap_high),
        8: (far_spread, swap_far),
        9: (near[0] + near[1] + near[2], swap_low),
        10: (far_rows + far[0] + far[1] + far[2], swap_rest),
    }
    pieces_sent = before_groups + [item for _, leaving in plan.values() for item in leaving]

    def start_all(pieces):
        for item in pieces:
            piece(*item).start()

    def wait_all(pieces):
        for item in pieces:
            piece(*item).wait_recv()

    def drain(pieces):
        for item in pieces:
            piece(*item).wait_send()

    local[0].wait()
    key = lax.broadcasted_iota(jnp.int32, (CH, CH), 0)
    lane = lax.broadcasted_iota(jnp.int32, (CH, CH), 1)
    order = jnp.where(key == 4 * (lane & 127) + (lane >> 7), 1.0, 0.0).astype(BF16)
    own_start = pl.multiple_of(r * SHARD, 16)
    for part in range(3):
        cw[pl.ds(own_start + 288 * part, 288), :] = jnp.dot(
            shard[pl.ds(288 * part, 288), :], order, preferred_element_type=F32
        ).astype(BF16)
    start_all(before_groups)

    def reorder(count, size):
        shape = (16 * size, count * 192)
        row = lax.broadcasted_iota(jnp.int32, shape, 0)
        col = lax.broadcasted_iota(jnp.int32, shape, 1)
        frame = row >> 4
        if size == 48:
            frame = (row * 21846) >> 20
        elif size == 32:
            frame = row >> 5
        place = row - frame * size
        strip = (place * 171) >> 11
        across = place - strip * 12
        wanted = (across & 1) * (count * 96) + strip * 96 + (across >> 1) * 16 + frame
        return jnp.where(jnp.logical_and(place < 12 * count, col == wanted), 1.0, 0.0).astype(BF16)

    perm4[...] = reorder(4, 48)
    perm2[...] = reorder(2, 32)
    row = lax.broadcasted_iota(jnp.int32, (ROWS, 8 * PAD), 0)
    col = lax.broadcasted_iota(jnp.int32, (ROWS, 8 * PAD), 1)
    strip = (row * 683) >> 16
    place = row - strip * 96
    which = (place * 171) >> 11
    wanted = which * PAD + strip * 12 + place - which * 12
    back[...] = jnp.where(col == wanted, 1.0, 0.0).astype(BF16)

    for copy in local[4:]:
        copy.wait()

    def attend(h):
        span = lanes(h * HEAD, HEAD)
        keys = win[1, :, :, :, :, span].reshape(ROWS, HEAD)
        values = win[2, :, :, :, :, span].reshape(ROWS, HEAD)
        for part in range(2):
            queries = win[0, pl.ds(2 * part, 2), :, :, :, span].reshape(ROWS // 2, HEAD)
            scores = lax.dot_general(
                queries, keys, (((1,), (1,)), ((), ())), preferred_element_type=F32
            ) * (1.0 / math.sqrt(HEAD))
            highest = jnp.max(scores, axis=-1, keepdims=True)
            weights = jnp.exp(scores - highest)
            probs = (weights * (1.0 / jnp.sum(weights, axis=-1, keepdims=True))).astype(BF16)
            mixed = jnp.dot(probs, values, preferred_element_type=F32).astype(BF16)
            att[pl.ds(2 * part, 2), :, :, :, span] = mixed.reshape(2, 3, 3, 16, HEAD)

    def await_home(g):
        for t in range(3):
            give(g, t).wait_recv()
        keep(g).wait()

    def add_pair(g, first):
        await_home(g)
        await_home(g + 1)
        rows = home[:, :, :, lanes(g * WIDE, 2 * WIDE)].reshape(ROWS, 2 * WIDE)

        def chunk(n, carry):
            span = lanes(n * CHUNK, CHUNK)
            product = jnp.dot(
                rows, wo[pl.ds(pl.multiple_of(g * WIDE, WIDE), 2 * WIDE), span], preferred_element_type=F32
            )
            base = tok[:, span].astype(F32) if first else res[:, :, :, span].reshape(ROWS, CHUNK)
            res[:, :, :, span] = (base + product).reshape(6, 6, 16, CHUNK)
            return carry

        lax.fori_loop(0, D // CHUNK, chunk, 0)
        acc[...] += jnp.dot(rows, both[0], preferred_element_type=F32).reshape(6, 6, 16, CH)

    last = GROUPS - 2

    def merge(g, slot):
        both[slot] = jnp.dot(
            wo[pl.ds(pl.multiple_of(g * WIDE, WIDE), 2 * WIDE), :], wp[...], preferred_element_type=F32
        ).astype(BF16)

    def project():
        acc[...] = jnp.zeros_like(acc)

        def chunk(n, carry):
            rows = pl.ds(pl.multiple_of(n * CHUNK, CHUNK), CHUNK)
            own = tok[:, lanes(n * CHUNK, CHUNK)]
            acc[...] += jnp.dot(own, wp[rows, :], preferred_element_type=F32).reshape(6, 6, 16, CH)
            return carry

        lax.fori_loop(0, D // CHUNK, chunk, 0)

    def group(g, carry):
        @pl.when(g < GROUPS - WINDOW)
        def _():
            for n in range(3):
                for t in range(3):
                    send(g, n, t).wait_send()
            send_group(g + WINDOW)

        @pl.when(g == 1)
        def _():
            for copy in local[1:4]:
                copy.wait()
            project()
            merge(last, 1)

        @pl.when(jnp.logical_and(g > 1, lax.rem(g, 2) == 0))
        def _():
            merge(g - 2, 0)

        @pl.when(g == 3)
        def _():
            add_pair(0, True)

        @pl.when(jnp.logical_and(g > 3, lax.rem(g, 2) == 1))
        def _():
            add_pair(g - 3, False)

        for n in range(3):
            for t in range(3):
                send(g, n, t).wait_recv()

        for h in range(WIDE // HEAD):
            attend(g * (WIDE // HEAD) + h)
        for t in ORDER:
            give(g, t).start()
        keep(g).start()

        def weights_step(arriving, leaving):
            def _():
                wait_all(arriving)
                start_all(leaving)

            return _

        for at_group, (arriving, leaving) in plan.items():
            pl.when(g == at_group)(weights_step(arriving, leaving))

        return carry

    lax.fori_loop(0, GROUPS, group, 0)

    await_home(last)
    await_home(last + 1)
    def rim(i):
        dr, dc = around[i]
        take = [pl.ds(1, 6) if d == 0 else (1 if d < 0 else 6) for d in (dr, dc)]
        put = pl.ds(1, 6) if dr == 0 else (7 if dr < 0 else 0)
        there = field.at[put, pl.ds(1, 6)] if dc == 0 else side.at[1 if dc < 0 else 0, put]
        return pltpu.make_async_remote_copy(
            src_ref=field.at[take[0], take[1]], dst_ref=there,
            send_sem=hs.at[i], recv_sem=hr.at[i],
            device_id=at(r + dr, c + dc), device_id_type=MESH,
        )

    def cells(ref, blocks, span):
        taken = [ref[pl.ds(i, m), pl.ds(j, n), :, span] for i, m, j, n in blocks]
        taken = [block.reshape(-1, block.shape[-1]) for block in taken]
        return taken[0] if len(taken) == 1 else jnp.concatenate(taken, axis=0)

    def finish(blocks):
        count = 16 * sum(m * n for _, m, _, n in blocks)
        rows = cells(home, blocks, pl.ds(last * WIDE, 2 * WIDE))

        def chunk(n, squares):
            span = lanes(n * CHUNK, CHUNK)
            total = cells(res, blocks, span) + jnp.dot(
                rows, wo[pl.ds(last * WIDE, 2 * WIDE), span], preferred_element_type=F32
            )
            for lane in range(0, CHUNK, 128):
                squares += total[:, lane : lane + 128] * total[:, lane : lane + 128]
            return squares

        squares = lax.fori_loop(0, D // CHUNK, chunk, jnp.zeros((count, 128), F32))
        mean = jnp.sum(squares, axis=-1, keepdims=True) * (1.0 / D)
        raw = cells(acc, blocks, pl.ds(0, CH)) + jnp.dot(rows, both[1], preferred_element_type=F32)
        raw = raw * lax.rsqrt(mean + 1e-6)
        features = (raw / (1.0 + jnp.exp(-raw))).astype(BF16)
        start = 0
        for i, m, j, n in blocks:
            size = 16 * m * n
            field[pl.ds(1 + i, m), pl.ds(1 + j, n)] = features[start : start + size].reshape(m, n, 16, CH)
            start += size

    sides = (0, 2, 3, 4, 5, 7)
    finish(((0, 6, 0, 1), (0, 6, 5, 1), (0, 1, 1, 4), (5, 1, 1, 4)))
    for i in (1, 6) + sides:
        rim(i).start()
    finish(((1, 4, 1, 4),))
    wait_all(swaps)
    def tap_rows(dt, dy, dx):
        return pl.ds(pl.multiple_of(((dt * 3 + dy) * 3 + dx) * CH, CH), CH)

    def middle(dt, carry):
        total = jnp.zeros((ROWS, CH), F32)
        for dx in range(3):
            total += jnp.dot(
                field[pl.ds(1, 6), pl.ds(dx, 6)].reshape(ROWS, CH), cw[tap_rows(dt, 1, dx), :],
                preferred_element_type=F32,
            )
        res[:, :, :, lanes(dt * 256, 256)] = total[:, :256].reshape(6, 6, 16, 256)
        res[:, :, :, lanes((dt + 3) * 256, 256)] = total[:, 256:].reshape(6, 6, 16, 256)
        return carry

    lax.fori_loop(0, 3, middle, 0)

    for i in (1, 6):
        rim(i).wait()

    @pl.when(r == 0)
    def _():
        field[0, pl.ds(1, 6)] = jnp.zeros((6, 16, CH), BF16)

    @pl.when(r == 15)
    def _():
        field[7, pl.ds(1, 6)] = jnp.zeros((6, 16, CH), BF16)

    def take_sides():
        for i in sides:
            rim(i).wait()

        @pl.when(r == 0)
        def _():
            side[:, 0] = jnp.zeros((2, 16, CH), BF16)

        @pl.when(r == 15)
        def _():
            side[:, 7] = jnp.zeros((2, 16, CH), BF16)

        @pl.when(c == 0)
        def _():
            side[0] = jnp.zeros((8, 16, CH), BF16)

        @pl.when(c == 7)
        def _():
            side[1] = jnp.zeros((8, 16, CH), BF16)

    def to_y(a, step):
        there = whose_y(step)
        return pltpu.make_async_remote_copy(
            src_ref=sent.at[a, pl.ds(4 * there, 4)], dst_ref=mid.at[a, y],
            send_sem=os_.at[a, step], recv_sem=or_.at[a, step], device_id=along_y(step), device_id_type=MESH,
        )

    def hop(a, step, e):
        origin = whose_y(step)
        block = sent.at[a, 4 * y + e] if step == 0 else mid.at[a, origin, e]
        return origin, block

    def mine(origin, e):
        return jnp.logical_and(own_corner, jnp.logical_and(origin == x, e == 2 * zl + odd))

    def to_owner(a, step, e):
        origin, block = hop(a, step, e)
        return pltpu.make_async_remote_copy(
            src_ref=block, dst_ref=got.at[a, odd, c], send_sem=cs.at[a, 4 * step + e], recv_sem=cr.at[a, odd, c],
            device_id=(4 * y + e, 2 * origin + zl), device_id_type=MESH,
        )

    def own(a, step, e):
        _, block = hop(a, step, e)
        return pltpu.make_async_copy(block, got.at[a, odd, c], cr.at[a, odd, c])

    def arrival(a, half, col):
        return pltpu.make_async_remote_copy(
            src_ref=sent.at[a, 0], dst_ref=got.at[a, half, col], send_sem=cs.at[a, 0], recv_sem=cr.at[a, half, col],
            device_id=other_core, device_id_type=MESH,
        )

    def spread(a, step):
        for e in range(4):
            @pl.when(mine(whose_y(step), e))
            def _(e=e):
                own(a, step, e).start()

            @pl.when(jnp.logical_not(mine(whose_y(step), e)))
            def _(e=e):
                to_owner(a, step, e).start()

    age = lax.broadcasted_iota(jnp.int32, (ROWS, 256), 0) & 15

    def convolve(a):
        def tap(dt, carry):
            spot = lanes((a * 3 + dt) * 256, 256)
            total = res[:, :, :, spot].reshape(ROWS, 256)
            for dy in (0, 2):
                for dx in range(3):
                    total += jnp.dot(
                        field[pl.ds(dy, 6), pl.ds(dx, 6)].reshape(ROWS, CH),
                        cw[tap_rows(dt, dy, dx), pl.ds(a * 256, 256)],
                        preferred_element_type=F32,
                    )
            res[:, :, :, spot] = total.reshape(6, 6, 16, 256)
            return carry

        lax.fori_loop(0, 3, tap, 0)
        if a == 0:
            take_sides()

        def edge(dt, carry):
            spot = lanes((a * 3 + dt) * 256, 256)
            for e, (j, dx) in enumerate(((0, 0), (5, 2))):
                total = res[:, j, :, spot].reshape(96, 256)
                for dy in range(3):
                    total += jnp.dot(
                        side[e, pl.ds(dy, 6)].reshape(96, CH), cw[tap_rows(dt, dy, dx), pl.ds(a * 256, 256)],
                        preferred_element_type=F32,
                    )
                res[:, j, :, spot] = total.reshape(6, 16, 256)
            return carry

        lax.fori_loop(0, 3, edge, 0)
        taps = [res[:, :, :, pl.ds((a * 3 + dt) * 256, 256)].reshape(ROWS, 256) for dt in range(3)]
        conv = taps[2]
        conv += jnp.where(age >= 1, pltpu.roll(taps[1], 1, axis=0), 0.0)
        conv += jnp.where(age >= 2, pltpu.roll(taps[0], 2, axis=0), 0.0)
        done = conv.astype(BF16)
        for rows, table, start, size in ((done[:384], perm4, 0, 48), (done[384:], perm2, 48, 32)):
            stacked = jnp.concatenate([rows[:, :128], rows[:, 128:]], axis=0)
            moved = jnp.dot(table[...], stacked, preferred_element_type=F32).astype(BF16)
            sent[a, :, pl.ds(start, size), :] = moved.reshape(16, size, 128)

        for step in (2, 1, 3):
            to_y(a, step).start()
        spread(a, 0)

    def pass_on(a):
        for step in (1, 3, 2):
            to_y(a, 4 - step).wait_recv()
            spread(a, step)

    def collect(a):
        for half in range(2):
            for col in range(8):
                arrival(a, half, col).wait_recv()
        for half in range(2):
            block = jnp.dot(
                back[...], got[a, half].reshape(8 * PAD, 128), preferred_element_type=F32
            ).astype(BF16)
            for i in range(6):
                out_ref[12 * half + 2 * i + a] = block[96 * i : 96 * i + 96]

    convolve(0)
    convolve(1)
    pass_on(0)
    pass_on(1)
    collect(0)
    collect(1)

    def drain_group(g, carry):
        @pl.when(g >= GROUPS - WINDOW)
        def _():
            for n in range(3):
                for t in range(3):
                    send(g, n, t).wait_send()

        for t in range(3):
            give(g, t).wait_send()
        return carry

    lax.fori_loop(0, GROUPS, drain_group, 0)
    drain(pieces_sent)

    for a in range(2):
        for step in range(4):
            if step:
                to_y(a, step).wait_send()
            for e in range(4):
                @pl.when(jnp.logical_not(mine(whose_y(step), e)))
                def _(a=a, step=step, e=e):
                    to_owner(a, step, e).wait_send()


def local(queries, keys, values, tokens, out_weight, proj_weight, conv_weight):
    cells = [jnp.transpose(a, (1, 2, 0, 3)) for a in (queries, keys, values)]
    rows = jnp.transpose(tokens, (1, 2, 0, 3)).reshape(ROWS, D)
    anywhere = pl.BlockSpec(memory_space=pl.ANY)
    dma = pltpu.SemaphoreType.DMA
    out = pl.pallas_call(
        body,
        out_shape=jax.ShapeDtypeStruct((24, 96, 128), BF16),
        in_specs=[anywhere] * 7,
        out_specs=pl.BlockSpec(memory_space=pltpu.VMEM),
        scratch_shapes=[
            pltpu.VMEM((3, 4, 3, 3, 16, INNER), BF16),
            pltpu.VMEM((4, 3, 3, 16, INNER), BF16),
            pltpu.VMEM((6, 6, 16, INNER), BF16),
            pltpu.VMEM((6, 6, 16, D), F32),
            pltpu.VMEM((ROWS, D), BF16),
            pltpu.VMEM((INNER, D), BF16),
            pltpu.VMEM((D, CH), BF16),
            pltpu.VMEM((16 * SHARD, CH), BF16),
            pltpu.VMEM((SHARD, CH), BF16),
            pltpu.VMEM((8, 8, 16, CH), BF16),
            pltpu.VMEM((2, 8, 16, CH), BF16),
            pltpu.VMEM((6, 6, 16, CH), F32),
            pltpu.VMEM((768, 768), BF16),
            pltpu.VMEM((512, 384), BF16),
            pltpu.VMEM((ROWS, 8 * PAD), BF16),
            pltpu.VMEM((2, 16, PAD, 128), BF16),
            pltpu.VMEM((2, 4, 4, PAD, 128), BF16),
            pltpu.VMEM((2, 2, 8, PAD, 128), BF16),
            pltpu.VMEM((2, 2 * WIDE, CH), BF16),
            dma((GROUPS, 3, 3)), dma((GROUPS, 3, 3)),
            dma((GROUPS, 3)), dma((GROUPS, 4)),
            dma((7,)),
            dma((48,)), dma((48,)),
            dma((8,)), dma((8,)),
            dma((2, 4)), dma((2, 4)),
            dma((2, 16)), dma((2, 2, 8)),
        ],
        compiler_params=pltpu.CompilerParams(
            collective_id=0, has_side_effects=True, vmem_limit_bytes=62 * 1024 * 1024
        ),
    )(*cells, rows, out_weight, proj_weight, conv_weight)
    return out[None]


def solution(mesh):
    tile = P(None, "row", "col", None)
    placed = (tile, tile, tile, tile, P(), P(), P("row", None))
    return jax.shard_map(
        local, mesh=mesh, in_specs=placed, out_specs=P("row", "col", None, None), check_vma=False
    )
```

```python
import math

import jax
import jax.numpy as jnp
from jax import lax
from jax.experimental import pallas as pl
from jax.experimental.pallas import tpu as pltpu
from jax.sharding import PartitionSpec as P

MESH = pl.DeviceIdType.MESH
HEADS = 12
HEAD = 128
GROUPS = 12
WIDE = 128
WINDOW = 2
ORDER = (0, 1, 2)
PAD = 80
INNER = 1536
D = 3072
CH = 512
SHARD = 864
HALF = 432
ROWS = 576
CHUNK = 512
F32 = jnp.float32
BF16 = jnp.bfloat16


def lanes(start, size):
    return pl.ds(pl.multiple_of(start, 128), size)


def body(q_ref, k_ref, v_ref, t_ref, wo_ref, wp_ref, cw_ref, out_ref,
         win, att, home, res, tok, wo, wp, cw, shard, field, side, acc, perm4, perm2, back, sent, mid, got, both,
         fs, fr, rs, rr, ls, ws, wr, hs, hr, os_, or_, cs, cr):
    r = lax.axis_index("row")
    c = lax.axis_index("col")
    odd = lax.rem(r, 2)
    x, zh = lax.div(c, 2), lax.rem(c, 2)
    y, zl = lax.div(r, 4), lax.rem(lax.div(r, 2), 2)

    def at(row, col):
        return (lax.rem(row + 16, 16), lax.rem(col + 8, 8))

    def along_x(step):
        return (r, lax.rem(x + step, 4) * 2 + zh)

    def along_y(step):
        return (lax.rem(y + step, 4) * 4 + zl * 2 + odd, c)

    other_zl = (y * 4 + (1 - zl) * 2 + odd, c)
    other_core = (r + 1 - 2 * odd, c)
    forward = (at(r - 1, c - odd), at(r - 1, c + 1 - odd), at(r, c - 1 + 2 * odd))
    homes = (at(r + 1, c + 1 - odd), at(r + 1, c - odd), at(r, c + 1 - 2 * odd))
    around = [(dr, dc) for dr in (-1, 0, 1) for dc in (-1, 0, 1) if (dr, dc) != (0, 0)]

    barrier = pltpu.get_barrier_semaphore()

    def greet(device):
        pl.semaphore_signal(barrier, inc=1, device_id=device, device_id_type=MESH)

    for dr, dc in around:
        greet(at(r + dr, c + dc))
    for step in (1, 2, 3):
        greet(along_x(step))
        greet(along_y(step))
    greet(other_zl)
    greet(other_core)
    own_corner = zl == zh
    for half in range(2):
        for col in range(8):
            row = 4 * y + 2 * zh + half

            @pl.when(jnp.logical_or(row != r, col != c))
            def _(row=row, col=col):
                greet((row, col))

    local = [
        pltpu.make_async_copy(cw_ref, shard, ls.at[0]),
        pltpu.make_async_copy(t_ref, tok, ls.at[1]),
        pltpu.make_async_copy(wo_ref, wo, ls.at[2]),
        pltpu.make_async_copy(wp_ref, wp, ls.at[3]),
    ]
    sources = (q_ref, k_ref, v_ref)
    for n in range(3):
        local.append(
            pltpu.make_async_copy(
                sources[n].at[pl.ds(3, 3), pl.ds(3 * (1 - odd), 3)], win.at[n, odd], ls.at[4 + n]
            )
        )
    local[0].start()
    for copy in local[4:]:
        copy.start()
    for j in (0, 7):
        field[:, j] = jnp.zeros((8, 16, CH), BF16)

    pl.semaphore_wait(barrier, 32 - own_corner.astype(jnp.int32))

    def send(g, n, t):
        span = lanes(g * WIDE, WIDE)
        if t == 2:
            src = sources[n].at[pl.ds(3, 3), pl.ds(3 * odd, 3), :, span]
            dst = win.at[n, 1 - odd, :, :, :, span]
        else:
            src = sources[n].at[pl.ds(0, 3), pl.ds(3 * t, 3), :, span]
            dst = win.at[n, 3 - t, :, :, :, span]
        return pltpu.make_async_remote_copy(
            src_ref=src, dst_ref=dst, send_sem=fs.at[g, n, t], recv_sem=fr.at[g, n, t],
            device_id=forward[t], device_id_type=MESH,
        )

    def give(g, t):
        span = lanes(g * WIDE, WIDE)
        if t == 2:
            src = att.at[1 - odd, :, :, :, span]
            dst = home.at[pl.ds(3, 3), pl.ds(3 * odd, 3), :, span]
        else:
            src = att.at[3 - t, :, :, :, span]
            dst = home.at[pl.ds(0, 3), pl.ds(3 * t, 3), :, span]
        return pltpu.make_async_remote_copy(
            src_ref=src, dst_ref=dst, send_sem=rs.at[g, t], recv_sem=rr.at[g, t],
            device_id=homes[t], device_id_type=MESH,
        )

    def keep(g):
        span = lanes(g * WIDE, WIDE)
        return pltpu.make_async_copy(
            att.at[odd, :, :, :, span], home.at[pl.ds(3, 3), pl.ds(3 * (1 - odd), 3), :, span], rr.at[g, 3]
        )

    def send_group(g):
        for n in range(3):
            for t in ORDER:
                send(g, n, t).start()

    for g in range(WINDOW):
        send_group(g)
    for copy in local[1:4]:
        copy.start()

    quarter = lanes(x * 128, 128)
    everything = pl.ds(0, CH)

    def piece(i, y_, zl_, part, span, device):
        first, size = part
        start = pl.multiple_of((y_ * 4 + zl_ * 2 + odd) * SHARD + first, 16)
        block = cw.at[pl.ds(start, size), span]
        return pltpu.make_async_remote_copy(
            src_ref=block, dst_ref=block, send_sem=ws.at[i], recv_sem=wr.at[i],
            device_id=device, device_id_type=MESH,
        )

    def whose_y(step):
        return lax.rem(y + step, 4)

    low, high, full = (0, HALF), (HALF, HALF), (0, SHARD)
    steps = (1, 3, 2)
    cross = [(0, y, zl, full, quarter, other_zl)]
    own_low = [(s, y, zl, low, quarter, along_y(s)) for s in steps]
    own_high = [(3 + s, y, zl, high, everything, along_y(s)) for s in steps]
    far_low = [(6 + s, y, 1 - zl, low, quarter, along_y(s)) for s in steps]
    far_high = [(9 + s, y, 1 - zl, high, quarter, along_x(s)) for s in steps]
    far_spread = [(12 + s, y, 1 - zl, low, quarter, along_x(s)) for s in steps]
    near = [[(12 + 3 * d + s, whose_y(d), zl, low, quarter, along_x(s)) for s in steps] for d in (1, 2, 3)]
    far_rows = [(24 + s, y, 1 - zl, high, everything, along_y(s)) for s in steps]
    far = [[(24 + 3 * d + s, whose_y(d), 1 - zl, low, quarter, along_x(s)) for s in steps] for d in (1, 2, 3)]
    swap_own = [(37, y, zl, full, everything, other_core)]
    swap_high = [(37 + d, whose_y(d), zl, high, everything, other_core) for d in (1, 2, 3)]
    swap_far = [(41, y, 1 - zl, full, everything, other_core)]
    swap_low = [(41 + d, whose_y(d), zl, low, everything, other_core) for d in (1, 2, 3)]
    swap_rest = [(44 + d, whose_y(d), 1 - zl, full, everything, other_core) for d in (1, 2, 3)]
    swaps = swap_own + swap_high + swap_far + swap_low + swap_rest
    before_groups = cross + own_low + swap_own
    plan = {
        0: ([], own_high[:1]),
        1: (cross, far_low + far_high + own_high[1:2]),
        2: (own_low, far_spread + near[0] + own_high[2:]),
        3: ([], near[1] + near[2]),
        4: (far_high, far_rows[:1]),
        5: (far_low, far_rows[1:2] + far[0]),
        6: ([], far_rows[2:] + far[1]),
        7: (own_high, far[2] + swap_high),
        8: (far_spread, swap_far),
        9: (near[0] + near[1] + near[2], swap_low),
        10: (far_rows + far[0] + far[1] + far[2], swap_rest),
    }
    pieces_sent = before_groups + [item for _, leaving in plan.values() for item in leaving]

    def start_all(pieces):
        for item in pieces:
            piece(*item).start()

    def wait_all(pieces):
        for item in pieces:
            piece(*item).wait_recv()

    def drain(pieces):
        for item in pieces:
            piece(*item).wait_send()

    local[0].wait()
    key = lax.broadcasted_iota(jnp.int32, (CH, CH), 0)
    lane = lax.broadcasted_iota(jnp.int32, (CH, CH), 1)
    order = jnp.where(key == 4 * (lane & 127) + (lane >> 7), 1.0, 0.0).astype(BF16)
    own_start = pl.multiple_of(r * SHARD, 16)
    for part in range(3):
        cw[pl.ds(own_start + 288 * part, 288), :] = jnp.dot(
            shard[pl.ds(288 * part, 288), :], order, preferred_element_type=F32
        ).astype(BF16)
    start_all(before_groups)

    def reorder(count, size):
        shape = (16 * size, count * 192)
        row = lax.broadcasted_iota(jnp.int32, shape, 0)
        col = lax.broadcasted_iota(jnp.int32, shape, 1)
        frame = row >> 4
        if size == 48:
            frame = (row * 21846) >> 20
        elif size == 32:
            frame = row >> 5
        place = row - frame * size
        strip = (place * 171) >> 11
        across = place - strip * 12
        wanted = (across & 1) * (count * 96) + strip * 96 + (across >> 1) * 16 + frame
        return jnp.where(jnp.logical_and(place < 12 * count, col == wanted), 1.0, 0.0).astype(BF16)

    perm4[...] = reorder(4, 48)
    perm2[...] = reorder(2, 32)
    row = lax.broadcasted_iota(jnp.int32, (ROWS, 8 * PAD), 0)
    col = lax.broadcasted_iota(jnp.int32, (ROWS, 8 * PAD), 1)
    strip = (row * 683) >> 16
    place = row - strip * 96
    which = (place * 171) >> 11
    wanted = which * PAD + strip * 12 + place - which * 12
    back[...] = jnp.where(col == wanted, 1.0, 0.0).astype(BF16)

    for copy in local[4:]:
        copy.wait()

    def attend(h):
        span = lanes(h * HEAD, HEAD)
        keys = win[1, :, :, :, :, span].reshape(ROWS, HEAD)
        values = win[2, :, :, :, :, span].reshape(ROWS, HEAD)
        for part in range(2):
            queries = win[0, pl.ds(2 * part, 2), :, :, :, span].reshape(ROWS // 2, HEAD)
            scores = lax.dot_general(
                queries, keys, (((1,), (1,)), ((), ())), preferred_element_type=F32
            ) * (1.0 / math.sqrt(HEAD))
            highest = jnp.max(scores, axis=-1, keepdims=True)
            weights = jnp.exp(scores - highest)
            probs = (weights * (1.0 / jnp.sum(weights, axis=-1, keepdims=True))).astype(BF16)
            mixed = jnp.dot(probs, values, preferred_element_type=F32).astype(BF16)
            att[pl.ds(2 * part, 2), :, :, :, span] = mixed.reshape(2, 3, 3, 16, HEAD)

    def await_home(g):
        for t in range(3):
            give(g, t).wait_recv()
        keep(g).wait()

    def add_pair(g, first):
        await_home(g)
        await_home(g + 1)
        rows = home[:, :, :, lanes(g * WIDE, 2 * WIDE)].reshape(ROWS, 2 * WIDE)

        def chunk(n, carry):
            span = lanes(n * CHUNK, CHUNK)
            product = jnp.dot(
                rows, wo[pl.ds(pl.multiple_of(g * WIDE, WIDE), 2 * WIDE), span], preferred_element_type=F32
            )
            base = tok[:, span].astype(F32) if first else res[:, :, :, span].reshape(ROWS, CHUNK)
            res[:, :, :, span] = (base + product).reshape(6, 6, 16, CHUNK)
            return carry

        lax.fori_loop(0, D // CHUNK, chunk, 0)
        acc[...] += jnp.dot(rows, both[0], preferred_element_type=F32).reshape(6, 6, 16, CH)

    last = GROUPS - 2

    def merge(g, slot):
        both[slot] = jnp.dot(
            wo[pl.ds(pl.multiple_of(g * WIDE, WIDE), 2 * WIDE), :], wp[...], preferred_element_type=F32
        ).astype(BF16)

    def project():
        acc[...] = jnp.zeros_like(acc)

        def chunk(n, carry):
            rows = pl.ds(pl.multiple_of(n * CHUNK, CHUNK), CHUNK)
            own = tok[:, lanes(n * CHUNK, CHUNK)]
            acc[...] += jnp.dot(own, wp[rows, :], preferred_element_type=F32).reshape(6, 6, 16, CH)
            return carry

        lax.fori_loop(0, D // CHUNK, chunk, 0)

    def group(g, carry):
        @pl.when(g < GROUPS - WINDOW)
        def _():
            for n in range(3):
                for t in range(3):
                    send(g, n, t).wait_send()
            send_group(g + WINDOW)

        @pl.when(g == 1)
        def _():
            for copy in local[1:4]:
                copy.wait()
            project()
            merge(last, 1)

        @pl.when(jnp.logical_and(g > 1, lax.rem(g, 2) == 0))
        def _():
            merge(g - 2, 0)

        @pl.when(g == 3)
        def _():
            add_pair(0, True)

        @pl.when(jnp.logical_and(g > 3, lax.rem(g, 2) == 1))
        def _():
            add_pair(g - 3, False)

        for n in range(3):
            for t in range(3):
                send(g, n, t).wait_recv()

        for h in range(WIDE // HEAD):
            attend(g * (WIDE // HEAD) + h)
        for t in ORDER:
            give(g, t).start()
        keep(g).start()

        def weights_step(arriving, leaving):
            def _():
                wait_all(arriving)
                start_all(leaving)

            return _

        for at_group, (arriving, leaving) in plan.items():
            pl.when(g == at_group)(weights_step(arriving, leaving))

        return carry

    lax.fori_loop(0, GROUPS, group, 0)

    await_home(last)
    await_home(last + 1)
    def rim(i):
        dr, dc = around[i]
        take = [pl.ds(1, 6) if d == 0 else (1 if d < 0 else 6) for d in (dr, dc)]
        put = pl.ds(1, 6) if dr == 0 else (7 if dr < 0 else 0)
        there = field.at[put, pl.ds(1, 6)] if dc == 0 else side.at[1 if dc < 0 else 0, put]
        return pltpu.make_async_remote_copy(
            src_ref=field.at[take[0], take[1]], dst_ref=there,
            send_sem=hs.at[i], recv_sem=hr.at[i],
            device_id=at(r + dr, c + dc), device_id_type=MESH,
        )

    def cells(ref, blocks, span):
        taken = [ref[pl.ds(i, m), pl.ds(j, n), :, span] for i, m, j, n in blocks]
        taken = [block.reshape(-1, block.shape[-1]) for block in taken]
        return taken[0] if len(taken) == 1 else jnp.concatenate(taken, axis=0)

    def finish(blocks):
        count = 16 * sum(m * n for _, m, _, n in blocks)
        rows = cells(home, blocks, pl.ds(last * WIDE, 2 * WIDE))

        def chunk(n, squares):
            span = lanes(n * (2 * CHUNK), (2 * CHUNK))
            total = cells(res, blocks, span) + jnp.dot(
                rows, wo[pl.ds(last * WIDE, 2 * WIDE), span], preferred_element_type=F32
            )
            for lane in range(0, (2 * CHUNK), 128):
                squares += total[:, lane : lane + 128] * total[:, lane : lane + 128]
            return squares

        squares = lax.fori_loop(0, D // (2 * CHUNK), chunk, jnp.zeros((count, 128), F32))
        mean = jnp.sum(squares, axis=-1, keepdims=True) * (1.0 / D)
        raw = cells(acc, blocks, pl.ds(0, CH)) + jnp.dot(rows, both[1], preferred_element_type=F32)
        raw = raw * lax.rsqrt(mean + 1e-6)
        features = (raw / (1.0 + jnp.exp(-raw))).astype(BF16)
        start = 0
        for i, m, j, n in blocks:
            size = 16 * m * n
            field[pl.ds(1 + i, m), pl.ds(1 + j, n)] = features[start : start + size].reshape(m, n, 16, CH)
            start += size

    sides = (0, 2, 3, 4, 5, 7)
    finish(((0, 6, 0, 6),))
    for i in (1, 6) + sides:
        rim(i).start()
    wait_all(swaps)
    def tap_rows(dt, dy, dx):
        return pl.ds(pl.multiple_of(((dt * 3 + dy) * 3 + dx) * CH, CH), CH)

    def middle(dt, carry):
        total = jnp.zeros((ROWS, CH), F32)
        for dx in range(3):
            total += jnp.dot(
                field[pl.ds(1, 6), pl.ds(dx, 6)].reshape(ROWS, CH), cw[tap_rows(dt, 1, dx), :],
                preferred_element_type=F32,
            )
        res[:, :, :, lanes(dt * 256, 256)] = total[:, :256].reshape(6, 6, 16, 256)
        res[:, :, :, lanes((dt + 3) * 256, 256)] = total[:, 256:].reshape(6, 6, 16, 256)
        return carry

    lax.fori_loop(0, 3, middle, 0)

    for i in (1, 6):
        rim(i).wait()

    @pl.when(r == 0)
    def _():
        field[0, pl.ds(1, 6)] = jnp.zeros((6, 16, CH), BF16)

    @pl.when(r == 15)
    def _():
        field[7, pl.ds(1, 6)] = jnp.zeros((6, 16, CH), BF16)

    def take_sides():
        for i in sides:
            rim(i).wait()

        @pl.when(r == 0)
        def _():
            side[:, 0] = jnp.zeros((2, 16, CH), BF16)

        @pl.when(r == 15)
        def _():
            side[:, 7] = jnp.zeros((2, 16, CH), BF16)

        @pl.when(c == 0)
        def _():
            side[0] = jnp.zeros((8, 16, CH), BF16)

        @pl.when(c == 7)
        def _():
            side[1] = jnp.zeros((8, 16, CH), BF16)

    def to_y(a, step):
        there = whose_y(step)
        return pltpu.make_async_remote_copy(
            src_ref=sent.at[a, pl.ds(4 * there, 4)], dst_ref=mid.at[a, y],
            send_sem=os_.at[a, step], recv_sem=or_.at[a, step], device_id=along_y(step), device_id_type=MESH,
        )

    def hop(a, step, e):
        origin = whose_y(step)
        block = sent.at[a, 4 * y + e] if step == 0 else mid.at[a, origin, e]
        return origin, block

    def mine(origin, e):
        return jnp.logical_and(own_corner, jnp.logical_and(origin == x, e == 2 * zl + odd))

    def to_owner(a, step, e):
        origin, block = hop(a, step, e)
        return pltpu.make_async_remote_copy(
            src_ref=block, dst_ref=got.at[a, odd, c], send_sem=cs.at[a, 4 * step + e], recv_sem=cr.at[a, odd, c],
            device_id=(4 * y + e, 2 * origin + zl), device_id_type=MESH,
        )

    def own(a, step, e):
        _, block = hop(a, step, e)
        return pltpu.make_async_copy(block, got.at[a, odd, c], cr.at[a, odd, c])

    def arrival(a, half, col):
        return pltpu.make_async_remote_copy(
            src_ref=sent.at[a, 0], dst_ref=got.at[a, half, col], send_sem=cs.at[a, 0], recv_sem=cr.at[a, half, col],
            device_id=other_core, device_id_type=MESH,
        )

    def spread(a, step):
        for e in range(4):
            @pl.when(mine(whose_y(step), e))
            def _(e=e):
                own(a, step, e).start()

            @pl.when(jnp.logical_not(mine(whose_y(step), e)))
            def _(e=e):
                to_owner(a, step, e).start()

    age = lax.broadcasted_iota(jnp.int32, (ROWS, 256), 0) & 15

    def convolve(a):
        def tap(dt, carry):
            spot = lanes((a * 3 + dt) * 256, 256)
            total = res[:, :, :, spot].reshape(ROWS, 256)
            for dy in (0, 2):
                for dx in range(3):
                    total += jnp.dot(
                        field[pl.ds(dy, 6), pl.ds(dx, 6)].reshape(ROWS, CH),
                        cw[tap_rows(dt, dy, dx), pl.ds(a * 256, 256)],
                        preferred_element_type=F32,
                    )
            res[:, :, :, spot] = total.reshape(6, 6, 16, 256)
            return carry

        lax.fori_loop(0, 3, tap, 0)
        if a == 0:
            take_sides()

        def edge(dt, carry):
            spot = lanes((a * 3 + dt) * 256, 256)
            for e, (j, dx) in enumerate(((0, 0), (5, 2))):
                total = res[:, j, :, spot].reshape(96, 256)
                for dy in range(3):
                    total += jnp.dot(
                        side[e, pl.ds(dy, 6)].reshape(96, CH), cw[tap_rows(dt, dy, dx), pl.ds(a * 256, 256)],
                        preferred_element_type=F32,
                    )
                res[:, j, :, spot] = total.reshape(6, 16, 256)
            return carry

        lax.fori_loop(0, 3, edge, 0)
        taps = [res[:, :, :, pl.ds((a * 3 + dt) * 256, 256)].reshape(ROWS, 256) for dt in range(3)]
        conv = taps[2]
        conv += jnp.where(age >= 1, pltpu.roll(taps[1], 1, axis=0), 0.0)
        conv += jnp.where(age >= 2, pltpu.roll(taps[0], 2, axis=0), 0.0)
        done = conv.astype(BF16)
        for rows, table, start, size in ((done[:384], perm4, 0, 48), (done[384:], perm2, 48, 32)):
            stacked = jnp.concatenate([rows[:, :128], rows[:, 128:]], axis=0)
            moved = jnp.dot(table[...], stacked, preferred_element_type=F32).astype(BF16)
            sent[a, :, pl.ds(start, size), :] = moved.reshape(16, size, 128)

        for step in (2, 1, 3):
            to_y(a, step).start()
        spread(a, 0)

    def pass_on(a):
        for step in (1, 3, 2):
            to_y(a, 4 - step).wait_recv()
            spread(a, step)

    def collect(a):
        for half in range(2):
            for col in range(8):
                arrival(a, half, col).wait_recv()
        for half in range(2):
            block = jnp.dot(
                back[...], got[a, half].reshape(8 * PAD, 128), preferred_element_type=F32
            ).astype(BF16)
            for i in range(6):
                out_ref[12 * half + 2 * i + a] = block[96 * i : 96 * i + 96]

    convolve(0)
    convolve(1)
    pass_on(0)
    pass_on(1)
    collect(0)
    collect(1)

    def drain_group(g, carry):
        @pl.when(g >= GROUPS - WINDOW)
        def _():
            for n in range(3):
                for t in range(3):
                    send(g, n, t).wait_send()

        for t in range(3):
            give(g, t).wait_send()
        return carry

    lax.fori_loop(0, GROUPS, drain_group, 0)
    drain(pieces_sent)

    for a in range(2):
        for step in range(4):
            if step:
                to_y(a, step).wait_send()
            for e in range(4):
                @pl.when(jnp.logical_not(mine(whose_y(step), e)))
                def _(a=a, step=step, e=e):
                    to_owner(a, step, e).wait_send()


def local(queries, keys, values, tokens, out_weight, proj_weight, conv_weight):
    cells = [jnp.transpose(a, (1, 2, 0, 3)) for a in (queries, keys, values)]
    rows = jnp.transpose(tokens, (1, 2, 0, 3)).reshape(ROWS, D)
    anywhere = pl.BlockSpec(memory_space=pl.ANY)
    dma = pltpu.SemaphoreType.DMA
    out = pl.pallas_call(
        body,
        out_shape=jax.ShapeDtypeStruct((24, 96, 128), BF16),
        in_specs=[anywhere] * 7,
        out_specs=pl.BlockSpec(memory_space=pltpu.VMEM),
        scratch_shapes=[
            pltpu.VMEM((3, 4, 3, 3, 16, INNER), BF16),
            pltpu.VMEM((4, 3, 3, 16, INNER), BF16),
            pltpu.VMEM((6, 6, 16, INNER), BF16),
            pltpu.VMEM((6, 6, 16, D), F32),
            pltpu.VMEM((ROWS, D), BF16),
            pltpu.VMEM((INNER, D), BF16),
            pltpu.VMEM((D, CH), BF16),
            pltpu.VMEM((16 * SHARD, CH), BF16),
            pltpu.VMEM((SHARD, CH), BF16),
            pltpu.VMEM((8, 8, 16, CH), BF16),
            pltpu.VMEM((2, 8, 16, CH), BF16),
            pltpu.VMEM((6, 6, 16, CH), F32),
            pltpu.VMEM((768, 768), BF16),
            pltpu.VMEM((512, 384), BF16),
            pltpu.VMEM((ROWS, 8 * PAD), BF16),
            pltpu.VMEM((2, 16, PAD, 128), BF16),
            pltpu.VMEM((2, 4, 4, PAD, 128), BF16),
            pltpu.VMEM((2, 2, 8, PAD, 128), BF16),
            pltpu.VMEM((2, 2 * WIDE, CH), BF16),
            dma((GROUPS, 3, 3)), dma((GROUPS, 3, 3)),
            dma((GROUPS, 3)), dma((GROUPS, 4)),
            dma((7,)),
            dma((48,)), dma((48,)),
            dma((8,)), dma((8,)),
            dma((2, 4)), dma((2, 4)),
            dma((2, 16)), dma((2, 2, 8)),
        ],
        compiler_params=pltpu.CompilerParams(
            collective_id=0, has_side_effects=True, vmem_limit_bytes=62 * 1024 * 1024
        ),
    )(*cells, rows, out_weight, proj_weight, conv_weight)
    return out[None]


def solution(mesh):
    tile = P(None, "row", "col", None)
    placed = (tile, tile, tile, tile, P(), P(), P("row", None))
    return jax.shard_map(
        local, mesh=mesh, in_specs=placed, out_specs=P("row", "col", None, None), check_vma=False
    )
```
